32 devices in a mesh: dp: 2 (over y), expert: 16 (over z, x, core).
Axes of the slice: x: 2, y: 2, z: 4, core: 2. Of those that a mesh axis runs over, the one named last changes fastest.
Arguments:
- tokens: bfloat16 [1024, 2048], P('expert', 'dp'), may hold values from -6 to 6
- expert_ids: int32 [1024, 8], P('expert'), may hold values from 0 to 31, all different within a row; in each aligned block of 64 rows (0 to 63, 64 to 127, ...) at most 24 rows name the same one
- route_weights: bfloat16 [1024, 8], P('expert'), may hold values from 0.019897461 to 0.3984375
- w_gate: bfloat16 [32, 2048, 1024], P('expert', None, 'dp'), may hold values from -0.125 to 0.125
- w_up: bfloat16 [32, 2048, 1024], P('expert', None, 'dp'), may hold values from -0.125 to 0.125
- w_down: bfloat16 [32, 1024, 2048], P('expert', 'dp'), may hold values from -0.1875 to 0.1875
Outputs:
- moe_out: bfloat16 [1024, 2048], P('expert', 'dp')
The draws below stay inside these ranges and needn't reach their ends.
Inputs may be any that keep to these rules, and one draw needn't show every extreme that they name: `expert_ids`: each token names 8 different experts. In each aligned block of 64 rows no expert is named more than 24 times, a bound that some block reaches.
All inputs are finite; a program needn't handle non-finite values.
Results may differ from the reference program's by a relative error of at most 0.019.
Values may be sent and summed in bfloat16 or wider, within the bound.
No kernel may reach another device: no remote copies, remote signals or barrier semaphores. Data moves between devices by JAX's collectives and lax.ppermute only.
A program may use at most 64 MiB of HBM per device.

```python
import math
import jax
import jax.numpy as jnp
import numpy as np
from jax import lax

D = 2048
FF = 1024
TOP_K = 8
TOK_DEV = 64
EXPERTS = 32
CAP = 24
TOKENS = 1024
N_DP = 2
N_EXPERT = 16


def shard_levels(own_key, extent, pieces, smallest, high):
    gain, own = 1.0, jax.random.fold_in(own_key, 6)
    for dim, blocks in pieces:
        draws = jnp.exp(jax.random.uniform(jax.random.fold_in(own, dim), (blocks,), jnp.float32, smallest / len(pieces), high / len(pieces)))
        gain = gain * jnp.repeat(draws, extent[dim] // blocks).reshape([-1 if axis == dim else 1 for axis in range(len(extent))])
    return gain


def shared_out(rng, own, number, rows, number_of, top, most, slope):
    ranking = jax.random.permutation(rng, number_of)
    packed, usual = shares(number_of, rows * top, most, slope, True), shares(number_of, rows * top, most, slope, False)
    places = jnp.arange(number_of)

    def named(lengths, turn):
        used = int((lengths > 0).sum())
        fixed = max(1, used // 4)
        moved = fixed + (places - fixed + turn * (used - fixed)) % max(1, number_of - fixed)
        return jnp.zeros((number_of,), jnp.int32).at[ranking[jnp.where(places < fixed, places, moved)]].set(jnp.asarray(lengths, jnp.int32))

    lengths = jnp.where(number % 4 == 0, named(packed, number // 4), named(usual, number - number // 4 - 1))
    mixed = jax.random.permutation(jax.random.fold_in(own, 3), number_of)
    giver, receiver = mixed[0:number_of // 2 * 2:2], mixed[1:number_of // 2 * 2:2]
    margin = jnp.minimum(lengths[giver] - 1, most - lengths[receiver]) // 2
    margin = jnp.where((giver == ranking[0]) | (receiver == ranking[0]) | (lengths[receiver] == 0), 0, jnp.maximum(margin, 0))
    moved = jax.random.randint(jax.random.fold_in(own, 4), (number_of // 2,), 0, 1 << 20) % (margin + 1)
    lengths = lengths.at[giver].add(-moved).at[receiver].add(moved)
    labels = jnp.searchsorted(jnp.cumsum(lengths), jnp.arange(rows * top), side="right").astype(jnp.int32)
    listing = labels.reshape(top, rows).T
    listing = listing[jax.random.permutation(jax.random.fold_in(own, 1), rows)]
    turn = jax.random.randint(jax.random.fold_in(own, 2), (rows, 1), 0, top)
    return jnp.take_along_axis(listing, (jnp.arange(top)[None, :] + turn) % top, axis=1)


def shares(count, total, reach, slope, full):
    weights = [(1 << 20) // math.isqrt(rank ** slope) + 1 for rank in range(1, count + 1)]
    largest = reach if full else min(reach, max(-(-total // count), total * weights[0] // sum(weights)))
    least = 1 if total - largest >= count - 1 else 0
    given, rest = [largest] + [least] * (count - 1), total - largest - least * (count - 1)
    while rest > 0:
        movable = [i for i in range(1, count) if given[i] < largest] or [i for i in range(1, count) if given[i] < reach]
        mass, left = sum([weights[i] for i in movable]), rest
        for i in movable:
            addition = min(reach - given[i], max(1, left * weights[i] // mass), rest)
            given[i] = given[i] + addition
            rest = rest - addition
    return np.array(given)


def centred(key, shape, width, reach, shards=(), kind=jnp.bfloat16):
    values = width * jax.random.normal(key, shape, jnp.float32)
    if shards:
        values = values * shard_levels(key, shape, shards, -0.22, 0.18)
    return jnp.clip(values, -reach, reach).astype(kind)


def setup_inputs(seed: int = 0) -> dict:
    splits = jax.random.split(jax.random.key(seed), 7)
    tokens = centred(splits[0], (TOKENS, D), 1.0, 6.0, ((0, 16), (1, 2)))
    expert_ids_keys = jax.random.split(jax.random.fold_in(splits[1], 1), TOKENS // TOK_DEV)
    expert_ids_turns = jax.random.permutation(jax.random.fold_in(splits[1], 3), TOKENS // TOK_DEV)
    expert_ids = jax.vmap(lambda own, number: shared_out(jax.random.fold_in(splits[1], 2), own, number, TOK_DEV, EXPERTS, TOP_K, CAP, 2))(expert_ids_keys, expert_ids_turns).reshape((TOKENS, TOP_K))
    route_weights = jnp.clip(jnp.exp(math.log(0.3984375) - 2.9969585 * jax.random.uniform(splits[2], (TOKENS, TOP_K), jnp.float32) ** shard_levels(splits[2], (TOKENS, TOP_K), ((0, 16),), -0.2, 0.2)), 0.019897461, 0.3984375).astype(jnp.bfloat16)
    w_gate = centred(splits[3], (EXPERTS, D, FF), D ** -0.5, 0.125, ((0, 16), (2, 2)))
    w_up = centred(splits[4], (EXPERTS, D, FF), D ** -0.5, 0.125, ((0, 16), (2, 2)))
    w_down = centred(splits[5], (EXPERTS, FF, D), FF ** -0.5, 0.1875, ((0, 16), (1, 2)))
    return {"tokens": tokens, "expert_ids": expert_ids, "route_weights": route_weights, "w_gate": w_gate, "w_up": w_up, "w_down": w_down}


def reference(tokens, expert_ids, route_weights, w_gate, w_up, w_down):
    flat_ids = expert_ids.reshape(-1).astype(jnp.int32)
    flat_weights = route_weights.reshape(-1).astype(jnp.float32)
    token_of = (jnp.arange(TOKENS * TOP_K, dtype=jnp.int32) // TOP_K).astype(jnp.int32)
    limit = N_EXPERT * CAP
    group_width = FF // N_DP

    def one_expert(total, expert_num):
        matches = flat_ids == expert_num
        picked = jnp.nonzero(matches, size=limit, fill_value=0)[0].astype(jnp.int32)
        live_rows = jnp.arange(limit, dtype=jnp.int32) < jnp.sum(matches.astype(jnp.int32))
        row_tokens = token_of[picked]
        rows = tokens[row_tokens]
        gate_proj = jnp.dot(rows, w_gate[expert_num], preferred_element_type=jnp.float32)
        up_proj = jnp.dot(rows, w_up[expert_num], preferred_element_type=jnp.float32)
        hidden = (jax.nn.silu(gate_proj) * up_proj).astype(jnp.bfloat16)
        hidden_groups = hidden.reshape(limit, N_DP, group_width).astype(jnp.float32)
        down_groups = w_down[expert_num].reshape(N_DP, group_width, D).astype(jnp.float32)
        partials = jnp.einsum("rgf,gfd->grd", hidden_groups, down_groups, precision=lax.Precision.HIGHEST)
        partials = lax.optimization_barrier(partials.astype(jnp.bfloat16)).astype(jnp.float32)
        scales = jnp.where(live_rows, flat_weights[picked], jnp.float32(0.0))
        terms = jnp.sum(partials * scales[None, :, None], axis=0)
        return total.at[row_tokens].add(terms), None

    start_total = jnp.zeros((TOKENS, D), jnp.float32)
    total, unused = lax.scan(one_expert, start_total, jnp.arange(EXPERTS, dtype=jnp.int32))
    return total.astype(jnp.bfloat16)
```

```python
import functools

import jax
import jax.numpy as jnp
from jax import lax
from jax.experimental import pallas as pl
from jax.experimental.pallas import tpu as pltpu
from jax.sharding import PartitionSpec as P

BF16, F32 = jnp.bfloat16, jnp.float32
PAIR = ("dp", "expert")
CHUNKS = 2
LANES = 128


def route_table(ids, weights, columns):
    lane = lax.broadcasted_iota(jnp.int32, (ids.shape[0], columns), 1)
    table = jnp.zeros((ids.shape[0], columns), F32)
    for k in range(ids.shape[1]):
        table = table + jnp.where(ids[:, k : k + 1] == lane, weights[:, k : k + 1].astype(F32), 0.0)
    return table


def pack_kernel(tok_ref, ids_ref, rw_ref, *outs):
    rows, width = tok_ref.shape
    table = route_table(ids_ref[...], rw_ref[...], outs[0].shape[1] - width).astype(BF16)
    part = rows // len(outs)
    for i, out in enumerate(outs):
        out[:, :width] = tok_ref[i * part : (i + 1) * part, :]
        out[:, width:] = table[i * part : (i + 1) * part, :]


def pack(tokens, ids, route_weights, columns):
    rows, width = tokens.shape
    one = jax.ShapeDtypeStruct((rows // CHUNKS, width + columns), BF16)
    return pl.pallas_call(pack_kernel, out_shape=[one] * CHUNKS)(tokens, ids, route_weights)


def join_kernel(*refs):
    *pieces, out, sem = refs
    rows = pieces[0].shape[0]
    copies = [
        pltpu.make_async_copy(piece, out.at[pl.ds(i * rows, rows)], sem.at[i])
        for i, piece in enumerate(pieces)
    ]
    for copy in copies:
        copy.start()
    for copy in copies:
        copy.wait()


def join(pieces):
    rows, width = pieces[0].shape
    return pl.pallas_call(
        join_kernel,
        in_specs=[pl.BlockSpec(memory_space=pl.ANY)] * len(pieces),
        out_specs=pl.BlockSpec(memory_space=pl.ANY),
        out_shape=jax.ShapeDtypeStruct((rows * len(pieces), width), BF16),
        scratch_shapes=[pltpu.SemaphoreType.DMA((len(pieces),))],
    )(*pieces)


def experts_kernel(places, gate_ref, up_ref, down_ref, *refs):
    pieces, (keep_ref, give_ref, rows_buf, table_buf, hidden_buf, sem) = refs[:-6], refs[-6:]
    step = pl.program_id(0)
    width = rows_buf.shape[1] // 2
    first_steps = hidden_buf.shape[1] // gate_ref.shape[2]
    per_expert = first_steps // 2
    row_count = rows_buf.shape[0]

    @pl.when(step == 0)
    def _():
        mine, others = places[0] * width, (1 - places[0]) * width
        copies, row = [], {0: 0, 1: 0}

        def fetch(source, target):
            copies.append(pltpu.make_async_copy(source, target, sem.at[len(copies)]))

        for core in range(2):
            own, by_x, by_y, diag_a, diag_b = pieces[5 * core : 5 * core + 5]
            for side, piece in ((0, own), (0, by_x), (1, by_y), (1, diag_a), (1, diag_b)):
                span = pl.ds(row[side], piece.shape[0])
                start = pl.multiple_of(others if side else mine, width)
                fetch(piece.at[:, pl.ds(0, width)], rows_buf.at[span, pl.ds(start, width)])
                if side == 0:
                    fetch(piece.at[:, pl.ds(width, table_buf.shape[1])], table_buf.at[span])
                row[side] += piece.shape[0]
        for copy in copies:
            copy.start()
        for copy in copies:
            copy.wait()

    @pl.when(step < first_steps)
    def _():
        rows = rows_buf[...]
        gate = jnp.dot(rows, gate_ref[0], preferred_element_type=F32)
        up = jnp.dot(rows, up_ref[0], preferred_element_type=F32)
        expert = places[1] * 2 + step // per_expert
        lane = lax.broadcasted_iota(jnp.int32, table_buf.shape, 1)
        weight = jnp.sum(
            jnp.where(lane == expert, table_buf[...].astype(F32), 0.0), axis=1, keepdims=True
        )
        hidden = gate / (1.0 + jnp.exp(-gate)) * up * weight
        columns = pl.ds(pl.multiple_of(step * gate_ref.shape[2], LANES), gate_ref.shape[2])
        hidden_buf[:, columns] = hidden.astype(BF16)

    @pl.when(step >= first_steps)
    def _():
        out = jnp.dot(hidden_buf[...], down_ref[...], preferred_element_type=F32).astype(BF16)
        keep_ref[0] = out[: row_count // 2]
        give_ref[0] = out[row_count // 2 :]


def run_experts(places, w_gate, w_up, w_down, pieces):
    experts, model, hidden = w_gate.shape
    width = model // 2
    rows = 2 * (pieces[0].shape[0] + pieces[1].shape[0])
    table = pieces[0].shape[1] - width
    step_hidden, step_out = hidden // 2, width // 2
    first, second = experts * 2, 4
    down = w_down.reshape(experts * hidden, model)

    def up_index(i, places):
        j = jnp.minimum(i, first - 1)
        return (j // 2, 0, j % 2)

    def down_index(i, places):
        j = jnp.maximum(i - first, 0)
        return (0, (j + places[0] * 2) % 4)

    def out_index(i, places):
        j = jnp.maximum(i - first, 0)
        return (j // 2, 0, j % 2)

    out = jax.ShapeDtypeStruct((2, rows // 2, width), BF16)
    return pl.pallas_call(
        experts_kernel,
        grid_spec=pltpu.PrefetchScalarGridSpec(
            num_scalar_prefetch=1,
            grid=(first + second,),
            in_specs=[
                pl.BlockSpec((1, model, step_hidden), up_index),
                pl.BlockSpec((1, model, step_hidden), up_index),
                pl.BlockSpec((experts * hidden, step_out), down_index),
            ]
            + [pl.BlockSpec(memory_space=pl.ANY)] * len(pieces),
            out_specs=[pl.BlockSpec((1, rows // 2, step_out), out_index)] * 2,
            scratch_shapes=[
                pltpu.VMEM((rows, model), BF16),
                pltpu.VMEM((rows, table), BF16),
                pltpu.VMEM((rows, experts * hidden), BF16),
                pltpu.SemaphoreType.DMA((14,)),
            ],
        ),
        out_shape=[out, out],
        compiler_params=pltpu.CompilerParams(vmem_limit_bytes=48 * 1024 * 1024),
        cost_estimate=pl.CostEstimate(
            flops=6 * rows * model * hidden * experts,
            bytes_accessed=6 * model * hidden * experts + 4 * rows * model,
            transcendentals=rows * hidden * experts,
        ),
    )(places, w_gate, w_up, down, *pieces)


def add(*terms):
    return functools.reduce(lambda a, b: a + b, [t.astype(F32) for t in terms]).astype(BF16)


def planned(peers, tokens, expert_ids, route_weights, w_gate, w_up, w_down):
    line = peers // 4

    def send(array, steps=0, x=0, core=0, y=0):
        pairs = []
        for side in range(2):
            for e in range(peers):
                to = (e // 4 + steps) % line * 4 + ((e // 2 % 2) ^ x) * 2 + ((e % 2) ^ core)
                pairs.append((side * peers + e, (side ^ y) * peers + to))
        return lax.ppermute(array, PAIR, pairs)

    expert_count = peers * w_gate.shape[0]
    columns = -(-expert_count // LANES) * LANES
    places = jnp.stack([lax.axis_index("dp"), lax.axis_index("expert")]).astype(jnp.int32)
    chunks = pack(tokens, expert_ids, route_weights, columns)

    def gather(chunk):
        own = join([chunk] + [send(chunk, steps=k) for k in range(1, line)])
        half = own.shape[0] // 2
        by_x, by_y = send(own, x=1), send(own, y=1)
        pieces = [own, by_x, by_y, send(by_x[:half], y=1), send(by_y[half:], x=1)]
        return pieces + [send(piece, core=1) for piece in pieces]

    def scatter(keep, give):
        total = add(keep, send(give, core=1))
        side, rows = total.shape[1] // 2, total.shape[1] // line // 2
        half = side // 2
        diag_a, diag_b = total[1, side : side + half], total[1, side + half :]
        got_a, got_b = send(diag_a, x=1), send(diag_b, y=1)
        for_x = jnp.concatenate([total[0, side : side + half], add(total[0, side + half :], got_b)], 0)
        for_y = jnp.concatenate([add(total[1, :half], got_a), total[1, half:side]], 0)
        mine = add(total[0, :side], send(for_x, x=1), send(for_y, y=1))
        back = [send(mine[k * rows : (k + 1) * rows], steps=line - k) for k in range(1, line)]
        return add(mine[:rows], *back)

    outs = []
    for chunk in chunks:
        outs.append(scatter(*run_experts(places, w_gate, w_up, w_down, gather(chunk))))
    return jnp.concatenate(outs, 0)


def general(tokens, expert_ids, route_weights, w_gate, w_up, w_down):
    peers, local = lax.axis_size("expert"), w_gate.shape[0]
    table = route_table(expert_ids, route_weights, peers * local).astype(BF16)
    rows = lax.all_gather(tokens, "expert", axis=0, tiled=True)
    rows = lax.all_gather(rows, "dp", axis=1, tiled=True)
    table = lax.all_gather(table, "expert", axis=0, tiled=True).astype(F32)
    weight = lax.dynamic_slice_in_dim(table, lax.axis_index("expert") * local, local, 1)
    gate = jnp.einsum("td,rdf->trf", rows, w_gate, preferred_element_type=F32)
    up = jnp.einsum("td,rdf->trf", rows, w_up, preferred_element_type=F32)
    hidden = (jax.nn.silu(gate) * up * weight[:, :, None]).astype(BF16)
    out = jnp.einsum("trf,rfd->td", hidden, w_down, preferred_element_type=F32).astype(BF16)
    out = lax.psum_scatter(out, "dp", scatter_dimension=1, tiled=True)
    return lax.psum_scatter(out, "expert", scatter_dimension=0, tiled=True)


def solution(mesh):
    peers = mesh.shape["expert"]
    body = general
    if mesh.shape["dp"] == 2 and peers % 4 == 0:
        body = functools.partial(planned, peers)
    return jax.shard_map(
        body,
        mesh=mesh,
        in_specs=(
            P("expert", "dp"),
            P("expert", None),
            P("expert", None),
            P("expert", None, "dp"),
            P("expert", None, "dp"),
            P("expert", "dp", None),
        ),
        out_specs=P("expert", "dp"),
        check_vma=False,
    )
```

```python
import functools

import jax
import jax.numpy as jnp
from jax import lax
from jax.experimental import pallas as pl
from jax.experimental.pallas import tpu as pltpu
from jax.sharding import PartitionSpec as P

BF16, F32 = jnp.bfloat16, jnp.float32
PAIR = ("dp", "expert")
CHUNKS = 2
LANES = 128
MIB = 1024 * 1024
VMEM_SPEC = pl.BlockSpec(memory_space=pltpu.VMEM)


def near(array):
    return pltpu.with_memory_space_constraint(array, pltpu.VMEM)


def route_table(ids, weights, experts):
    lane = lax.broadcasted_iota(jnp.int32, (ids.shape[0], experts), 1)
    table = jnp.zeros((ids.shape[0], experts), F32)
    for k in range(ids.shape[1]):
        table = table + jnp.where(ids[:, k : k + 1] == lane, weights[:, k : k + 1].astype(F32), 0.0)
    return table


def pack_kernel(tok_ref, ids_ref, rw_ref, *outs):
    rows, width = tok_ref.shape
    columns = outs[0].shape[1] - width
    line = lax.broadcasted_iota(jnp.int32, (columns, rows), 0)
    table = jnp.zeros((columns, rows), F32)
    for k in range(ids_ref.shape[0]):
        table = table + jnp.where(ids_ref[k : k + 1, :] == line, rw_ref[k : k + 1, :].astype(F32), 0.0)
    table = table.T.astype(BF16)
    part = rows // len(outs)
    for i, out in enumerate(outs):
        out[:, :width] = tok_ref[i * part : (i + 1) * part, :]
        out[:, width:] = table[i * part : (i + 1) * part, :]


def pack(tokens, ids, route_weights, columns):
    rows, width = tokens.shape
    one = jax.ShapeDtypeStruct((rows // CHUNKS, width + columns), BF16)
    return pl.pallas_call(
        pack_kernel,
        in_specs=[VMEM_SPEC] * 3,
        out_specs=[VMEM_SPEC] * CHUNKS,
        out_shape=[one] * CHUNKS,
        compiler_params=pltpu.CompilerParams(vmem_limit_bytes=2 * MIB),
    )(tokens, ids.T, route_weights.T)


def experts_kernel(first, counts, places, gate_in, up_in, down_in, *refs):
    if first:
        pieces, refs = refs[:-9], refs[-9:]
        keep_ref, give_ref, gate_ref, up_ref, down_ref, rows_buf, weight_buf, hidden_buf, sem = refs
    else:
        pieces, refs = refs[:-5], refs[-5:]
        keep_ref, give_ref, rows_buf, weight_buf, hidden_buf = refs
        gate_ref, up_ref, down_ref = gate_in, up_in, down_in
    experts, model, hidden = gate_ref.shape
    width = model // 2
    block, part = hidden // 2, width // 2
    steps = [(e, half) for e in range(experts) for half in range(2)]
    parts = [(side, half) for side in range(2) for half in range(2)]

    fetches = []
    if first:
        for e, half in steps:
            span = (e, slice(None), pl.ds(half * block, block))
            pair = [(gate_in.at[span], gate_ref.at[span]), (up_in.at[span], up_ref.at[span])]
            fetches.append(pair)
        for j in range(2):
            span = pl.ds(j * (experts * hidden // 2), experts * hidden // 2)
            fetches.append([(down_in.at[span], down_ref.at[span])])
        fetches = [
            [pltpu.make_async_copy(*ends, sem.at[2 * i + k]) for k, ends in enumerate(group)]
            for i, group in enumerate(fetches)
        ]
        for group in fetches:
            for copy in group:
                copy.start()

    mine = pl.ds(pl.multiple_of(places[0] * width, width), width)
    others = pl.ds(pl.multiple_of((1 - places[0]) * width, width), width)
    taken = 0
    for count, columns in zip(counts, (mine, others)):
        row = 0
        for piece in pieces[taken : taken + count]:
            span = pl.ds(row, piece.shape[0])
            rows_buf[span, columns] = piece[:, :width]
            if columns is mine:
                table = piece[:, width:].astype(F32)
                lane = lax.broadcasted_iota(jnp.int32, table.shape, 1)
                for e in range(experts):
                    hit = jnp.where(lane == places[1] * experts + e, table, 0.0)
                    weight_buf[e, span, :] = jnp.sum(hit, axis=1, keepdims=True)
            row += piece.shape[0]
        taken += count

    half_rows = rows_buf.shape[0] // 2
    for i, (e, half) in enumerate(steps):
        if first:
            for copy in fetches[i]:
                copy.wait()
        rows, span = rows_buf[...], pl.ds(half * block, block)
        gate = jnp.dot(rows, gate_ref[e, :, span], preferred_element_type=F32)
        up = jnp.dot(rows, up_ref[e, :, span], preferred_element_type=F32)
        value = gate / (1.0 + jnp.exp(-gate)) * up * weight_buf[e]
        hidden_buf[:, pl.ds(i * block, block)] = value.astype(BF16)
    if first:
        for group in fetches[len(steps) :]:
            for copy in group:
                copy.wait()
    for side, half in parts:
        at = pl.multiple_of((side + places[0]) % 2 * width + half * part, part)
        out = jnp.dot(hidden_buf[...], down_ref[:, pl.ds(at, part)], preferred_element_type=F32)
        keep_ref[side, :, pl.ds(half * part, part)] = out[:half_rows].astype(BF16)
        give_ref[side, :, pl.ds(half * part, part)] = out[half_rows:].astype(BF16)


def run_experts(places, weights, mine, others, first):
    experts, model, hidden = weights[0].shape
    width = model // 2
    rows = sum(piece.shape[0] for piece in mine)
    out = jax.ShapeDtypeStruct((2, rows // 2, width), BF16)
    where = pltpu.HBM if first else pltpu.VMEM
    operands = [pltpu.with_memory_space_constraint(w, where) for w in weights]
    operands += [near(piece) for piece in (*mine, *others)]
    specs = [pl.BlockSpec(memory_space=pl.ANY if first else pltpu.VMEM)] * 3
    specs += [VMEM_SPEC] * (len(operands) - 3)
    outs, extra = [out, out], []
    if first:
        outs += [jax.ShapeDtypeStruct(w.shape, BF16) for w in weights]
        extra = [pltpu.SemaphoreType.DMA((4 * experts + 4,))]
    return pl.pallas_call(
        functools.partial(experts_kernel, first, (len(mine), len(others))),
        in_specs=[pl.BlockSpec(memory_space=pltpu.SMEM)] + specs,
        out_specs=[VMEM_SPEC] * len(outs),
        scratch_shapes=[
            pltpu.VMEM((rows, model), BF16),
            pltpu.VMEM((experts, rows, 1), F32),
            pltpu.VMEM((rows, experts * hidden), BF16),
        ]
        + extra,
        out_shape=outs,
        compiler_params=pltpu.CompilerParams(vmem_limit_bytes=16 * MIB),
        cost_estimate=pl.CostEstimate(
            flops=6 * rows * model * hidden * experts,
            bytes_accessed=6 * model * hidden * experts + 4 * rows * model,
            transcendentals=rows * hidden * experts,
        ),
    )(places, *operands)


def add(*terms):
    return functools.reduce(lambda a, b: a + b, [t.astype(F32) for t in terms]).astype(BF16)


def planned(peers, tokens, expert_ids, route_weights, w_gate, w_up, w_down):
    line = peers // 4

    def send(array, steps=0, x=0, core=0, y=0):
        pairs = []
        for side in range(2):
            for e in range(peers):
                to = (e // 4 + steps) % line * 4 + ((e // 2 % 2) ^ x) * 2 + ((e % 2) ^ core)
                pairs.append((side * peers + e, (side ^ y) * peers + to))
        return lax.ppermute(array, PAIR, pairs)

    expert_count = peers * w_gate.shape[0]
    columns = -(-expert_count // LANES) * LANES
    places = jnp.stack([lax.axis_index("dp"), lax.axis_index("expert")]).astype(jnp.int32)
    chunks = pack(tokens, expert_ids, route_weights, columns)

    def join(pieces):
        return jnp.concatenate(pieces, 0)

    def cores(pieces):
        return [send(piece, core=1) for piece in pieces]

    def scatter(total, total_x):
        side, rows = total.shape[1], total.shape[1] // line
        half = side // 2
        got_a, got_b = send(total_x[1, :half], x=1), send(total_x[1, half:], y=1)
        for_x = join([total_x[0, :half], add(total_x[0, half:], got_b)])
        for_y = join([add(total[1, :half], got_a), total[1, half:]])
        mine = add(total[0], send(for_x, x=1), send(for_y, y=1))
        back = [send(mine[k * rows : (k + 1) * rows], steps=line - k) for k in range(1, line)]
        return add(mine[:rows], *back)

    weights = (w_gate, w_up, w_down.reshape(-1, w_down.shape[2]))
    first, outs = True, []
    for chunk in chunks:
        own = join([chunk] + [send(chunk, steps=k) for k in range(1, line)])
        half = own.shape[0] // 2
        by_x, by_y = send(own, x=1), send(own, y=1)
        diag = [send(by_x[:half], y=1), send(by_y[half:], x=1)]
        keep, give, *rest = run_experts(places, weights, [own] + cores([own]), [by_y] + cores([by_y]), first)
        if first:
            weights, first = rest, False
        total = add(keep, send(give, core=1))
        keep, give = run_experts(places, weights, [by_x] + cores([by_x]), diag + cores(diag), first)
        outs.append(scatter(total, add(keep, send(give, core=1))))
    return join(outs)


def general(tokens, expert_ids, route_weights, w_gate, w_up, w_down):
    peers, local = lax.axis_size("expert"), w_gate.shape[0]
    table = route_table(expert_ids, route_weights, peers * local).astype(BF16)
    rows = lax.all_gather(tokens, "expert", axis=0, tiled=True)
    rows = lax.all_gather(rows, "dp", axis=1, tiled=True)
    table = lax.all_gather(table, "expert", axis=0, tiled=True).astype(F32)
    weight = lax.dynamic_slice_in_dim(table, lax.axis_index("expert") * local, local, 1)
    gate = jnp.einsum("td,rdf->trf", rows, w_gate, preferred_element_type=F32)
    up = jnp.einsum("td,rdf->trf", rows, w_up, preferred_element_type=F32)
    hidden = (jax.nn.silu(gate) * up * weight[:, :, None]).astype(BF16)
    out = jnp.einsum("trf,rfd->td", hidden, w_down, preferred_element_type=F32).astype(BF16)
    out = lax.psum_scatter(out, "dp", scatter_dimension=1, tiled=True)
    return lax.psum_scatter(out, "expert", scatter_dimension=0, tiled=True)


def solution(mesh):
    peers = mesh.shape["expert"]
    body = general
    if mesh.shape["dp"] == 2 and peers % 4 == 0:
        body = functools.partial(planned, peers)
    return jax.shard_map(
        body,
        mesh=mesh,
        in_specs=(
            P("expert", "dp"),
            P("expert", None),
            P("expert", None),
            P("expert", None, "dp"),
            P("expert", None, "dp"),
            P("expert", "dp", None),
        ),
        out_specs=P("expert", "dp"),
        check_vma=False,
    )
```

```python
import functools

import jax
import jax.numpy as jnp
from jax import lax
from jax.experimental import pallas as pl
from jax.experimental.pallas import tpu as pltpu
from jax.sharding import PartitionSpec as P

BF16, F32 = jnp.bfloat16, jnp.float32
PAIR = ("dp", "expert")
LANES = 128
MIB = 1024 * 1024
VMEM_SPEC = pl.BlockSpec(memory_space=pltpu.VMEM)


def near(array):
    return pltpu.with_memory_space_constraint(array, pltpu.VMEM)


def route_table(ids, weights, experts):
    lane = lax.broadcasted_iota(jnp.int32, (ids.shape[0], experts), 1)
    table = jnp.zeros((ids.shape[0], experts), F32)
    for k in range(ids.shape[1]):
        table = table + jnp.where(ids[:, k : k + 1] == lane, weights[:, k : k + 1].astype(F32), 0.0)
    return table


def pack_kernel(tok_hbm, ids_hbm, rw_hbm, out_ref, ids_ref, rw_ref, sem):
    rows, width = tok_hbm.shape
    columns = out_ref.shape[1] - width
    ends = (ids_hbm, ids_ref), (rw_hbm, rw_ref), (tok_hbm, out_ref.at[:, pl.ds(0, width)])
    copies = [pltpu.make_async_copy(*pair, sem.at[i]) for i, pair in enumerate(ends)]
    for copy in copies:
        copy.start()
    for copy in copies[:2]:
        copy.wait()
    line = lax.broadcasted_iota(jnp.int32, (columns, rows), 0)
    table = jnp.zeros((columns, rows), F32)
    for k in range(ids_ref.shape[0]):
        table = table + jnp.where(ids_ref[k : k + 1, :] == line, rw_ref[k : k + 1, :].astype(F32), 0.0)
    out_ref[:, width:] = table.T.astype(BF16)
    copies[2].wait()


def pack(tokens, ids, route_weights, columns):
    rows, width = tokens.shape
    operands = [pltpu.with_memory_space_constraint(x, pltpu.HBM) for x in (tokens, ids.T, route_weights.T)]
    return pl.pallas_call(
        pack_kernel,
        in_specs=[pl.BlockSpec(memory_space=pl.ANY)] * 3,
        out_specs=VMEM_SPEC,
        out_shape=jax.ShapeDtypeStruct((rows, width + columns), BF16),
        scratch_shapes=[
            pltpu.VMEM(operands[1].shape, jnp.int32),
            pltpu.VMEM(operands[2].shape, BF16),
            pltpu.SemaphoreType.DMA((3,)),
        ],
        compiler_params=pltpu.CompilerParams(vmem_limit_bytes=2 * MIB),
    )(*operands)


def dispatch(table, expert_place, experts, block, room):
    rows = table.shape[0]
    this = lax.broadcasted_iota(jnp.int32, (rows, rows), 0)
    other = lax.broadcasted_iota(jnp.int32, (rows, rows), 1)
    before = (other < this) & (other // block == this // block)
    ranks = jnp.dot(before.astype(BF16), (table > 0.0).astype(BF16), preferred_element_type=F32)
    lane = lax.broadcasted_iota(jnp.int32, table.shape, 1)
    slots = experts * rows // block * room
    slot = lax.broadcasted_iota(jnp.int32, (rows, slots), 1)
    first = lax.broadcasted_iota(jnp.int32, (rows, 1), 0) // block * room
    taken = jnp.zeros((rows, slots), F32)
    for e in range(experts):
        here = lane == expert_place * experts + e
        weight = jnp.sum(jnp.where(here, table, 0.0), axis=1, keepdims=True)
        rank = jnp.sum(jnp.where(here, ranks, 0.0), axis=1, keepdims=True).astype(jnp.int32)
        taken = taken + jnp.where(slot == first + rank + e * (slots // experts), weight, 0.0)
    return taken


def experts_kernel(first, counts, block, room, places, gate_in, up_in, down_in, *refs):
    if first:
        pieces, refs = refs[:-13], refs[-13:]
        corner_keep, corner_give, keep_ref, give_ref, gate_ref, up_ref, down_ref, *refs, sem = refs
    else:
        pieces, refs = refs[:-9], refs[-9:]
        corner_keep, corner_give, keep_ref, give_ref, *refs = refs
        gate_ref, up_ref, down_ref = gate_in, up_in, down_in
    rows_buf, table_buf, taken_buf, packed_buf, out_buf = refs
    experts, model, hidden = gate_ref.shape
    width = model // 2
    fetches = []
    if first:
        ends = []
        for e in range(experts):
            span = pl.ds(e * hidden, hidden)
            ends += [(gate_in.at[e], gate_ref.at[e]), (up_in.at[e], up_ref.at[e])]
            ends += [(down_in.at[span], down_ref.at[span])]
        fetches = [pltpu.make_async_copy(*pair, sem.at[i]) for i, pair in enumerate(ends)]
        for copy in fetches:
            copy.start()

    mine = pl.ds(pl.multiple_of(places[0] * width, width), width)
    others = pl.ds(pl.multiple_of((1 - places[0]) * width, width), width)
    group = rows_buf.shape[0] // 2
    slots = taken_buf.shape[2] // experts
    taken = 0
    for g in range(2):
        for count, columns in zip(counts[g], (mine, others)):
            row = g * group
            for piece in pieces[taken : taken + count]:
                span = pl.ds(row, piece.shape[0])
                rows_buf[span, columns] = piece[:, :width]
                if columns is mine:
                    table_buf[span, :] = piece[:, width:].astype(F32)
                row += piece.shape[0]
            taken += count
        table = dispatch(table_buf[pl.ds(g * group, group), :], places[1], experts, block, room)
        taken_buf[g] = table.astype(BF16)
        picked = jnp.where(table > 0.0, 1.0, 0.0).T.astype(BF16)
        packed = jnp.dot(picked, rows_buf[pl.ds(g * group, group), :], preferred_element_type=F32).astype(BF16)
        for e in range(experts):
            packed_buf[e, pl.ds(g * slots, slots), :] = packed[e * slots : (e + 1) * slots]

    for e in range(experts):
        for copy in fetches[3 * e : 3 * e + 3]:
            copy.wait()
        rows = packed_buf[e]
        gate = jnp.dot(rows, gate_ref[e], preferred_element_type=F32)
        up = jnp.dot(rows, up_ref[e], preferred_element_type=F32)
        value = (gate / (1.0 + jnp.exp(-gate)) * up).astype(BF16)
        down = down_ref[pl.ds(e * hidden, hidden), :]
        out = jnp.dot(value, down, preferred_element_type=F32).astype(BF16)
        for g in range(2):
            out_buf[g, pl.ds(e * slots, slots), :] = out[g * slots : (g + 1) * slots]
    half = group // 2
    for g in (1, 0):
        for side, columns in enumerate((mine, others)):
            out = jnp.dot(taken_buf[g], out_buf[g, :, columns], preferred_element_type=F32).astype(BF16)
            if g and side:
                corner_keep[...] = out[:half]
                corner_give[...] = out[half:]
            else:
                keep_ref[g + 2 * side] = out[:half]
                give_ref[g + 2 * side] = out[half:]


def run_experts(places, weights, groups, block, room, first):
    experts, model, hidden = weights[0].shape
    width = model // 2
    rows = 2 * sum(piece.shape[0] for piece in groups[0][0])
    table = groups[0][0][0].shape[1] - width
    where = pltpu.HBM if first else pltpu.VMEM
    operands = [pltpu.with_memory_space_constraint(w, where) for w in weights]
    operands += [near(piece) for pair in groups for half in pair for piece in half]
    outs = [jax.ShapeDtypeStruct((rows // 4, width), BF16)] * 2
    outs += [jax.ShapeDtypeStruct((3, rows // 4, width), BF16)] * 2
    extra = []
    if first:
        outs += [jax.ShapeDtypeStruct(w.shape, BF16) for w in weights]
        extra = [pltpu.SemaphoreType.DMA((3 * experts,))]
    slots = rows // 2 // block * room
    counts = tuple(tuple(len(half) for half in pair) for pair in groups)
    return pl.pallas_call(
        functools.partial(experts_kernel, first, counts, block, room),
        in_specs=[pl.BlockSpec(memory_space=pltpu.SMEM)]
        + [pl.BlockSpec(memory_space=pl.ANY if first else pltpu.VMEM)] * 3
        + [VMEM_SPEC] * (len(operands) - 3),
        out_specs=[VMEM_SPEC] * len(outs),
        scratch_shapes=[
            pltpu.VMEM((rows, model), BF16),
            pltpu.VMEM((rows, table), F32),
            pltpu.VMEM((2, rows // 2, experts * slots), BF16),
            pltpu.VMEM((experts, 2 * slots, model), BF16),
            pltpu.VMEM((2, experts * slots, model), BF16),
        ]
        + extra,
        out_shape=outs,
        compiler_params=pltpu.CompilerParams(vmem_limit_bytes=20 * MIB),
        cost_estimate=pl.CostEstimate(flops=rows, bytes_accessed=rows, transcendentals=0),
    )(places, *operands)


def add(*terms):
    return functools.reduce(lambda a, b: a + b, [t.astype(F32) for t in terms]).astype(BF16)


def after(arrays, others):
    return lax.optimization_barrier((arrays, others))[0]


def planned(peers, tokens, expert_ids, route_weights, w_gate, w_up, w_down):
    line = peers // 4

    def send(array, steps=0, x=0, core=0, y=0):
        pairs = []
        for side in range(2):
            for e in range(peers):
                to = ((e // 4) ^ steps) * 4 + ((e // 2 % 2) ^ x) * 2 + ((e % 2) ^ core)
                pairs.append((side * peers + e, (side ^ y) * peers + to))
        return lax.ppermute(array, PAIR, pairs)

    expert_count = peers * w_gate.shape[0]
    columns = -(-expert_count // LANES) * LANES
    places = jnp.stack([lax.axis_index("dp"), lax.axis_index("expert")]).astype(jnp.int32)
    rows = pack(tokens, expert_ids, route_weights, columns)

    def join(pieces):
        return jnp.concatenate(pieces, 0)

    def cores(pieces):
        return [send(piece, core=1) for piece in pieces]

    def gather(own):
        half = own.shape[0] // 2
        by_x, by_y = send(own, x=1), send(own, y=1)
        corner = [send(by_x[:half], y=1), send(by_y[half:], x=1)]
        return [[own] + cores([own]), [by_y] + cores([by_y])], [[by_x] + cores([by_x]), corner + cores(corner)]

    def total(keep, give):
        return add(keep, send(give, core=1))

    def turn(corner, rest):
        for_x, for_y = rest[1], rest[2]
        half = for_x.shape[0] // 2
        got_a, got_b = send(corner[:half], x=1), send(corner[half:], y=1)
        for_x = join([for_x[:half], add(for_x[half:], got_b)])
        for_y = join([add(for_y[:half], got_a), for_y[half:]])
        return for_x, for_y

    weights = (w_gate, w_up, w_down.reshape(-1, w_down.shape[2]))
    block = tokens.shape[0]
    room = block * expert_ids.shape[1] * 3 // (2 * expert_count)
    blocks = [rows] + [send(rows, steps=k) for k in range(1, line)]
    parts, first, sums = 2, True, []
    count = line // parts
    for i in range(parts):
        groups = gather(join(blocks[i * count : (i + 1) * count]))
        corner, corner_give, keep, give, *rest = run_experts(places, weights, groups, block, room, first)
        if first:
            weights, first = rest, False
        rest = total(keep, give)
        sums.append((rest[0], *turn(total(corner, corner_give), rest)))
    back, arrived = [], ()
    for i in reversed(range(parts)):
        own, for_x, for_y = sums[i]
        for_x, for_y = after((for_x, for_y), arrived)
        arrived = send(for_x, x=1), send(for_y, y=1)
        mine = add(own, *arrived)
        for k in range(count):
            piece = mine[k * block : (k + 1) * block]
            back.append(send(piece, steps=i * count + k) if i or k else piece)
    return add(*back)


def general(tokens, expert_ids, route_weights, w_gate, w_up, w_down):
    peers, local = lax.axis_size("expert"), w_gate.shape[0]
    table = route_table(expert_ids, route_weights, peers * local).astype(BF16)
    rows = lax.all_gather(tokens, "expert", axis=0, tiled=True)
    rows = lax.all_gather(rows, "dp", axis=1, tiled=True)
    table = lax.all_gather(table, "expert", axis=0, tiled=True).astype(F32)
    weight = lax.dynamic_slice_in_dim(table, lax.axis_index("expert") * local, local, 1)
    gate = jnp.einsum("td,rdf->trf", rows, w_gate, preferred_element_type=F32)
    up = jnp.einsum("td,rdf->trf", rows, w_up, preferred_element_type=F32)
    hidden = (jax.nn.silu(gate) * up * weight[:, :, None]).astype(BF16)
    out = jnp.einsum("trf,rfd->td", hidden, w_down, preferred_element_type=F32).astype(BF16)
    out = lax.psum_scatter(out, "dp", scatter_dimension=1, tiled=True)
    return lax.psum_scatter(out, "expert", scatter_dimension=0, tiled=True)


def solution(mesh):
    peers = mesh.shape["expert"]
    body = general
    if mesh.shape["dp"] == 2 and peers % 8 == 0 and peers & (peers - 1) == 0:
        body = functools.partial(planned, peers)
    return jax.shard_map(
        body,
        mesh=mesh,
        in_specs=(
            P("expert", "dp"),
            P("expert", None),
            P("expert", None),
            P("expert", None, "dp"),
            P("expert", None, "dp"),
            P("expert", "dp", None),
        ),
        out_specs=P("expert", "dp"),
        check_vma=False,
    )
```

```python
import functools

import jax
import jax.numpy as jnp
from jax import lax
from jax.experimental import pallas as pl
from jax.experimental.pallas import tpu as pltpu
from jax.sharding import PartitionSpec as P

BF16, F32 = jnp.bfloat16, jnp.float32
PAIR = ("dp", "expert")
LANES = 128
GATHER = (True, False)
SCATTER = (False, False)
MIB = 1024 * 1024
VMEM_SPEC = pl.BlockSpec(memory_space=pltpu.VMEM)


def near(array):
    return pltpu.with_memory_space_constraint(array, pltpu.VMEM)


def route_table(ids, weights, experts):
    lane = lax.broadcasted_iota(jnp.int32, (ids.shape[0], experts), 1)
    table = jnp.zeros((ids.shape[0], experts), F32)
    for k in range(ids.shape[1]):
        table = table + jnp.where(ids[:, k : k + 1] == lane, weights[:, k : k + 1].astype(F32), 0.0)
    return table


def pack_kernel(tok_hbm, ids_hbm, rw_hbm, out_ref, ids_ref, rw_ref, sem):
    rows, width = tok_hbm.shape
    columns = out_ref.shape[1] - width
    ends = (ids_hbm, ids_ref), (rw_hbm, rw_ref), (tok_hbm, out_ref.at[:, pl.ds(0, width)])
    copies = [pltpu.make_async_copy(*pair, sem.at[i]) for i, pair in enumerate(ends)]
    for copy in copies:
        copy.start()
    for copy in copies[:2]:
        copy.wait()
    line = lax.broadcasted_iota(jnp.int32, (columns, rows), 0)
    table = jnp.zeros((columns, rows), F32)
    for k in range(ids_ref.shape[0]):
        table = table + jnp.where(ids_ref[k : k + 1, :] == line, rw_ref[k : k + 1, :].astype(F32), 0.0)
    out_ref[:, width:] = table.T.astype(BF16)
    copies[2].wait()


def pack(tokens, ids, route_weights, columns):
    rows, width = tokens.shape
    operands = [pltpu.with_memory_space_constraint(x, pltpu.HBM) for x in (tokens, ids.T, route_weights.T)]
    return pl.pallas_call(
        pack_kernel,
        in_specs=[pl.BlockSpec(memory_space=pl.ANY)] * 3,
        out_specs=VMEM_SPEC,
        out_shape=jax.ShapeDtypeStruct((rows, width + columns), BF16),
        scratch_shapes=[
            pltpu.VMEM(operands[1].shape, jnp.int32),
            pltpu.VMEM(operands[2].shape, BF16),
            pltpu.SemaphoreType.DMA((3,)),
        ],
        compiler_params=pltpu.CompilerParams(vmem_limit_bytes=2 * MIB),
    )(*operands)


def earlier(rows, block):
    this = lax.broadcasted_iota(jnp.int32, (rows, rows), 0)
    other = lax.broadcasted_iota(jnp.int32, (rows, rows), 1)
    start = jnp.zeros((rows, 1), jnp.int32)
    place = lax.broadcasted_iota(jnp.int32, (rows, 1), 0)
    for i in range(1, rows // block):
        start = jnp.where(place >= i * block, i * block, start)
    return ((other < this) & (other >= start)).astype(BF16)


def dispatch(table, before, expert_place, experts, block, room):
    rows = table.shape[0]
    ranks = jnp.dot(before, (table > 0.0).astype(BF16), preferred_element_type=F32)
    lane = lax.broadcasted_iota(jnp.int32, table.shape, 1)
    slots = experts * rows // block * room
    slot = lax.broadcasted_iota(jnp.int32, (rows, slots), 1)
    place = lax.broadcasted_iota(jnp.int32, (rows, 1), 0)
    first = jnp.zeros((rows, 1), jnp.int32)
    for i in range(1, rows // block):
        first = jnp.where(place >= i * block, i * room, first)
    taken = jnp.zeros((rows, slots), F32)
    for e in range(experts):
        here = lane == expert_place * experts + e
        weight = jnp.sum(jnp.where(here, table, 0.0), axis=1, keepdims=True)
        rank = jnp.sum(jnp.where(here, ranks, 0.0), axis=1, keepdims=True).astype(jnp.int32)
        taken = taken + jnp.where(slot == first + rank + e * (slots // experts), weight, 0.0)
    return taken


def experts_kernel(first, counts, block, room, places, gate_in, up_in, down_in, *refs):
    if first:
        pieces, refs = refs[:-14], refs[-14:]
        corner_keep, corner_give, keep_ref, give_ref, gate_ref, up_ref, down_ref, *refs, sem = refs
    else:
        pieces, refs = refs[:-10], refs[-10:]
        corner_keep, corner_give, keep_ref, give_ref, *refs = refs
        gate_ref, up_ref, down_ref = gate_in, up_in, down_in
    rows_buf, table_buf, taken_buf, packed_buf, out_buf, hidden_buf = refs
    experts, model, hidden = gate_ref.shape
    width = model // 2
    fetches = []
    if first:
        ends = []
        for e in range(experts):
            ends += [(gate_in.at[e], gate_ref.at[e]), (up_in.at[e], up_ref.at[e])]
        for e in range(experts):
            span = pl.ds(e * hidden, hidden)
            ends += [(down_in.at[span], down_ref.at[span])]
        fetches = [pltpu.make_async_copy(*pair, sem.at[i]) for i, pair in enumerate(ends)]
        for copy in fetches:
            copy.start()

    mine = pl.ds(pl.multiple_of(places[0] * width, width), width)
    others = pl.ds(pl.multiple_of((1 - places[0]) * width, width), width)
    group = rows_buf.shape[0] // 2
    slots = taken_buf.shape[2] // experts
    before = earlier(group, block)
    taken = 0
    for g in range(2):
        for count, columns in zip(counts[g], (mine, others)):
            row = g * group
            for piece in pieces[taken : taken + count]:
                span = pl.ds(row, piece.shape[0])
                rows_buf[span, columns] = piece[:, :width]
                if columns is mine:
                    table_buf[span, :] = piece[:, width:].astype(F32)
                row += piece.shape[0]
            taken += count
        table = dispatch(table_buf[pl.ds(g * group, group), :], before, places[1], experts, block, room)
        taken_buf[g] = table.astype(BF16)
        picked = jnp.where(table > 0.0, 1.0, 0.0).T.astype(BF16)
        packed = jnp.dot(picked, rows_buf[pl.ds(g * group, group), :], preferred_element_type=F32).astype(BF16)
        for e in range(experts):
            packed_buf[e, pl.ds(g * slots, slots), :] = packed[e * slots : (e + 1) * slots]

    for e in range(experts):
        for copy in fetches[2 * e : 2 * e + 2]:
            copy.wait()
        rows = packed_buf[e]
        gate = jnp.dot(rows, gate_ref[e], preferred_element_type=F32)
        up = jnp.dot(rows, up_ref[e], preferred_element_type=F32)
        hidden_buf[e] = (gate / (1.0 + jnp.exp(-gate)) * up).astype(BF16)
    for e in range(experts):
        for copy in fetches[2 * experts + e : 2 * experts + e + 1]:
            copy.wait()
        down = down_ref[pl.ds(e * hidden, hidden), :]
        out = jnp.dot(hidden_buf[e], down, preferred_element_type=F32).astype(BF16)
        for g in range(2):
            out_buf[g, pl.ds(e * slots, slots), :] = out[g * slots : (g + 1) * slots]
    half = group // 2
    for g in (1, 0):
        for side, columns in enumerate((mine, others)):
            out = jnp.dot(taken_buf[g], out_buf[g, :, columns], preferred_element_type=F32).astype(BF16)
            if g and side:
                corner_keep[...] = out[:half]
                corner_give[...] = out[half:]
            else:
                keep_ref[g + 2 * side] = out[:half]
                give_ref[g + 2 * side] = out[half:]


def run_experts(places, weights, groups, block, room, first):
    experts, model, hidden = weights[0].shape
    width = model // 2
    rows = 2 * sum(piece.shape[0] for piece in groups[0][0])
    table = groups[0][0][0].shape[1] - width
    where = pltpu.HBM if first else pltpu.VMEM
    operands = [pltpu.with_memory_space_constraint(w, where) for w in weights]
    operands += [near(piece) for pair in groups for half in pair for piece in half]
    outs = [jax.ShapeDtypeStruct((rows // 4, width), BF16)] * 2
    outs += [jax.ShapeDtypeStruct((3, rows // 4, width), BF16)] * 2
    extra = []
    if first:
        outs += [jax.ShapeDtypeStruct(w.shape, BF16) for w in weights]
        extra = [pltpu.SemaphoreType.DMA((3 * experts,))]
    slots = rows // 2 // block * room
    counts = tuple(tuple(len(half) for half in pair) for pair in groups)
    return pl.pallas_call(
        functools.partial(experts_kernel, first, counts, block, room),
        in_specs=[pl.BlockSpec(memory_space=pltpu.SMEM)]
        + [pl.BlockSpec(memory_space=pl.ANY if first else pltpu.VMEM)] * 3
        + [VMEM_SPEC] * (len(operands) - 3),
        out_specs=[VMEM_SPEC] * len(outs),
        scratch_shapes=[
            pltpu.VMEM((rows, model), BF16),
            pltpu.VMEM((rows, table), F32),
            pltpu.VMEM((2, rows // 2, experts * slots), BF16),
            pltpu.VMEM((experts, 2 * slots, model), BF16),
            pltpu.VMEM((2, experts * slots, model), BF16),
            pltpu.VMEM((experts, 2 * slots, hidden), BF16),
        ]
        + extra,
        out_shape=outs,
        compiler_params=pltpu.CompilerParams(vmem_limit_bytes=20 * MIB),
        cost_estimate=pl.CostEstimate(flops=rows, bytes_accessed=rows, transcendentals=0),
    )(places, *operands)


def cut_kernel(by_x, by_y, *refs):
    out_x, out_y = refs[-2:]
    half = out_x.shape[0]
    out_x[...] = by_x[:half, : out_x.shape[1]]
    out_y[...] = by_y[half:]


def cut(by_x, by_y, behind):
    half = jax.ShapeDtypeStruct((by_y.shape[0] // 2, by_y.shape[1]), BF16)
    return pl.pallas_call(
        cut_kernel,
        in_specs=[VMEM_SPEC] * 2 + [pl.BlockSpec(memory_space=pl.ANY)] * len(behind),
        out_specs=[VMEM_SPEC] * 2,
        out_shape=[half, half],
        compiler_params=pltpu.CompilerParams(vmem_limit_bytes=2 * MIB),
        cost_estimate=pl.CostEstimate(flops=1, bytes_accessed=1, transcendentals=0),
    )(near(by_x), near(by_y), *behind)


def add(*terms):
    return functools.reduce(lambda a, b: a + b, [t.astype(F32) for t in terms]).astype(BF16)


def after(arrays, others):
    return lax.optimization_barrier((arrays, others))[0]


def planned(peers, tokens, expert_ids, route_weights, w_gate, w_up, w_down):
    line = peers // 4

    def send(array, steps=0, x=0, core=0, y=0):
        pairs = []
        for side in range(2):
            for e in range(peers):
                to = ((e // 4) ^ steps) * 4 + ((e // 2 % 2) ^ x) * 2 + ((e % 2) ^ core)
                pairs.append((side * peers + e, (side ^ y) * peers + to))
        return lax.ppermute(array, PAIR, pairs)

    expert_count = peers * w_gate.shape[0]
    columns = -(-expert_count // LANES) * LANES
    places = jnp.stack([lax.axis_index("dp"), lax.axis_index("expert")]).astype(jnp.int32)
    rows = pack(tokens, expert_ids, route_weights, columns)

    def join(pieces):
        return jnp.concatenate(pieces, 0)

    def cores(pieces):
        return [send(piece, core=1) for piece in pieces]

    def gather(own, direct):
        features = own[:, : tokens.shape[1]]
        by_x, by_y = send(own, x=1), send(features, y=1)
        if direct:
            corner = [send(features, x=1, y=1)]
        else:
            half_x, half_y = cut(by_x, by_y, [])
            corner = [send(half_x, y=1), send(half_y, x=1)]
        return [[own] + cores([own]), [by_y] + cores([by_y])], [[by_x] + cores([by_x]), corner + cores(corner)]

    def total(keep, give):
        return add(keep, send(give, core=1))

    def turn(corner, rest):
        for_x, for_y = rest[1], rest[2]
        half = for_x.shape[0] // 2
        got_a, got_b = send(corner[:half], x=1), send(corner[half:], y=1)
        for_x = join([for_x[:half], add(for_x[half:], got_b)])
        for_y = join([add(for_y[:half], got_a), for_y[half:]])
        return for_x, for_y

    weights = (w_gate, w_up, w_down.reshape(-1, w_down.shape[2]))
    block = tokens.shape[0]
    room = block * expert_ids.shape[1] * 3 // (2 * expert_count)
    blocks = [rows] + [send(rows, steps=k) for k in range(1, line)]
    parts, first, sums = 2, True, []
    count = line // parts
    for i in range(parts):
        groups = gather(join(blocks[i * count : (i + 1) * count]), GATHER[i])
        corner, corner_give, keep, give, *rest = run_experts(places, weights, groups, block, room, first)
        if first:
            weights, first = rest, False
        rest = total(keep, give)
        corner = total(corner, corner_give)
        if SCATTER[i]:
            sums.append((rest[0], rest[1], rest[2], [send(corner, x=1, y=1)]))
        else:
            sums.append((rest[0], *turn(corner, rest), []))
    back, arrived = [], ()
    for i in reversed(range(parts)):
        own, for_x, for_y, direct = sums[i]
        for_x, for_y = after((for_x, for_y), arrived)
        arrived = send(for_x, x=1), send(for_y, y=1)
        mine = add(own, *arrived, *direct)
        for k in range(count):
            piece = mine[k * block : (k + 1) * block]
            back.append(send(piece, steps=i * count + k) if i or k else piece)
    return add(*back)


def general(tokens, expert_ids, route_weights, w_gate, w_up, w_down):
    peers, local = lax.axis_size("expert"), w_gate.shape[0]
    table = route_table(expert_ids, route_weights, peers * local).astype(BF16)
    rows = lax.all_gather(tokens, "expert", axis=0, tiled=True)
    rows = lax.all_gather(rows, "dp", axis=1, tiled=True)
    table = lax.all_gather(table, "expert", axis=0, tiled=True).astype(F32)
    weight = lax.dynamic_slice_in_dim(table, lax.axis_index("expert") * local, local, 1)
    gate = jnp.einsum("td,rdf->trf", rows, w_gate, preferred_element_type=F32)
    up = jnp.einsum("td,rdf->trf", rows, w_up, preferred_element_type=F32)
    hidden = (jax.nn.silu(gate) * up * weight[:, :, None]).astype(BF16)
    out = jnp.einsum("trf,rfd->td", hidden, w_down, preferred_element_type=F32).astype(BF16)
    out = lax.psum_scatter(out, "dp", scatter_dimension=1, tiled=True)
    return lax.psum_scatter(out, "expert", scatter_dimension=0, tiled=True)


def solution(mesh):
    peers = mesh.shape["expert"]
    body = general
    if mesh.shape["dp"] == 2 and peers % 8 == 0 and peers & (peers - 1) == 0:
        body = functools.partial(planned, peers)
    return jax.shard_map(
        body,
        mesh=mesh,
        in_specs=(
            P("expert", "dp"),
            P("expert", None),
            P("expert", None),
            P("expert", None, "dp"),
            P("expert", None, "dp"),
            P("expert", "dp", None),
        ),
        out_specs=P("expert", "dp"),
        check_vma=False,
    )
```

```python
import functools

import jax
import jax.numpy as jnp
from jax import lax
from jax.experimental import pallas as pl
from jax.experimental.pallas import tpu as pltpu
from jax.sharding import PartitionSpec as P

BF16, F32 = jnp.bfloat16, jnp.float32
PAIR = ("dp", "expert")
LANES = 128
GATHER = (True, False)
SCATTER = (False, False)
MIB = 1024 * 1024
VMEM_SPEC = pl.BlockSpec(memory_space=pltpu.VMEM)


def near(array):
    return pltpu.with_memory_space_constraint(array, pltpu.VMEM)


def route_table(ids, weights, experts):
    lane = lax.broadcasted_iota(jnp.int32, (ids.shape[0], experts), 1)
    table = jnp.zeros((ids.shape[0], experts), F32)
    for k in range(ids.shape[1]):
        table = table + jnp.where(ids[:, k : k + 1] == lane, weights[:, k : k + 1].astype(F32), 0.0)
    return table


def pack_kernel(tok_hbm, ids_hbm, rw_hbm, out_ref, ids_ref, rw_ref, sem):
    rows, width = tok_hbm.shape
    columns = out_ref.shape[1] - width
    ends = (ids_hbm, ids_ref), (rw_hbm, rw_ref), (tok_hbm, out_ref.at[:, pl.ds(0, width)])
    copies = [pltpu.make_async_copy(*pair, sem.at[i]) for i, pair in enumerate(ends)]
    for copy in copies:
        copy.start()
    for copy in copies[:2]:
        copy.wait()
    line = lax.broadcasted_iota(jnp.int32, (columns, rows), 0)
    table = jnp.zeros((columns, rows), F32)
    for k in range(ids_ref.shape[0]):
        table = table + jnp.where(ids_ref[k : k + 1, :] == line, rw_ref[k : k + 1, :].astype(F32), 0.0)
    out_ref[:, width:] = table.T.astype(BF16)
    copies[2].wait()


def pack(tokens, ids, route_weights, columns):
    rows, width = tokens.shape
    operands = [pltpu.with_memory_space_constraint(x, pltpu.HBM) for x in (tokens, ids.T, route_weights.T)]
    return pl.pallas_call(
        pack_kernel,
        in_specs=[pl.BlockSpec(memory_space=pl.ANY)] * 3,
        out_specs=VMEM_SPEC,
        out_shape=jax.ShapeDtypeStruct((rows, width + columns), BF16),
        scratch_shapes=[
            pltpu.VMEM(operands[1].shape, jnp.int32),
            pltpu.VMEM(operands[2].shape, BF16),
            pltpu.SemaphoreType.DMA((3,)),
        ],
        compiler_params=pltpu.CompilerParams(vmem_limit_bytes=2 * MIB),
    )(*operands)


def earlier(rows, block):
    this = lax.broadcasted_iota(jnp.int32, (rows, rows), 0)
    other = lax.broadcasted_iota(jnp.int32, (rows, rows), 1)
    start = jnp.zeros((rows, 1), jnp.int32)
    place = lax.broadcasted_iota(jnp.int32, (rows, 1), 0)
    for i in range(1, rows // block):
        start = jnp.where(place >= i * block, i * block, start)
    return ((other < this) & (other >= start)).astype(BF16)


def dispatch(table, before, expert_place, experts, block, room):
    rows = table.shape[0]
    ranks = jnp.dot(before, (table > 0.0).astype(BF16), preferred_element_type=F32)
    lane = lax.broadcasted_iota(jnp.int32, table.shape, 1)
    slots = experts * rows // block * room
    slot = lax.broadcasted_iota(jnp.int32, (rows, slots), 1)
    place = lax.broadcasted_iota(jnp.int32, (rows, 1), 0)
    first = jnp.zeros((rows, 1), jnp.int32)
    for i in range(1, rows // block):
        first = jnp.where(place >= i * block, i * room, first)
    taken = jnp.zeros((rows, slots), F32)
    for e in range(experts):
        here = lane == expert_place * experts + e
        weight = jnp.sum(jnp.where(here, table, 0.0), axis=1, keepdims=True)
        rank = jnp.sum(jnp.where(here, ranks, 0.0), axis=1, keepdims=True).astype(jnp.int32)
        taken = taken + jnp.where(slot == first + rank + e * (slots // experts), weight, 0.0)
    return taken


def experts_kernel(first, counts, block, room, places, gate_in, up_in, down_in, *refs):
    if first:
        pieces, refs = refs[:-14], refs[-14:]
        corner_keep, corner_give, keep_ref, give_ref, gate_ref, up_ref, down_ref, *refs, sem = refs
    else:
        pieces, refs = refs[:-10], refs[-10:]
        corner_keep, corner_give, keep_ref, give_ref, *refs = refs
        gate_ref, up_ref, down_ref = gate_in, up_in, down_in
    rows_buf, table_buf, taken_buf, packed_buf, out_buf, hidden_buf = refs
    experts, model, hidden = gate_ref.shape
    width = model // 2
    fetches = []
    if first:
        ends = []
        for e in range(experts):
            ends += [(gate_in.at[e], gate_ref.at[e]), (up_in.at[e], up_ref.at[e])]
        for e in range(experts):
            span = pl.ds(e * hidden, hidden)
            ends += [(down_in.at[span], down_ref.at[span])]
        fetches = [pltpu.make_async_copy(*pair, sem.at[i]) for i, pair in enumerate(ends)]
        for copy in fetches:
            copy.start()

    mine = pl.ds(pl.multiple_of(places[0] * width, width), width)
    others = pl.ds(pl.multiple_of((1 - places[0]) * width, width), width)
    group = rows_buf.shape[0] // 2
    slots = taken_buf.shape[2] // experts
    before = earlier(group, block)
    taken = 0
    for g in range(2):
        for count, columns in zip(counts[g], (mine, others)):
            row = g * group
            for piece in pieces[taken : taken + count]:
                span = pl.ds(row, piece.shape[0])
                rows_buf[span, columns] = piece[:, :width]
                if columns is mine:
                    table_buf[span, :] = piece[:, width:].astype(F32)
                row += piece.shape[0]
            taken += count
        table = dispatch(table_buf[pl.ds(g * group, group), :], before, places[1], experts, block, room)
        taken_buf[g] = table.astype(BF16)
        picked = jnp.where(table > 0.0, 1.0, 0.0).T.astype(BF16)
        packed = jnp.dot(picked, rows_buf[pl.ds(g * group, group), :], preferred_element_type=F32).astype(BF16)
        for e in range(experts):
            packed_buf[e, pl.ds(g * slots, slots), :] = packed[e * slots : (e + 1) * slots]

    for e in range(experts):
        for copy in fetches[2 * e : 2 * e + 2]:
            copy.wait()
        rows = packed_buf[e]
        gate = jnp.dot(rows, gate_ref[e], preferred_element_type=F32)
        up = jnp.dot(rows, up_ref[e], preferred_element_type=F32)
        hidden_buf[e] = (gate / (1.0 + jnp.exp(-gate)) * up).astype(BF16)
    for e in range(experts):
        for copy in fetches[2 * experts + e : 2 * experts + e + 1]:
            copy.wait()
        down = down_ref[pl.ds(e * hidden, hidden), :]
        out = jnp.dot(hidden_buf[e], down, preferred_element_type=F32).astype(BF16)
        for g in range(2):
            out_buf[g, pl.ds(e * slots, slots), :] = out[g * slots : (g + 1) * slots]
    half = group // 2
    for g in (1, 0):
        for side, columns in enumerate((mine, others)):
            out = jnp.dot(taken_buf[g], out_buf[g, :, columns], preferred_element_type=F32).astype(BF16)
            if g and side:
                corner_keep[...] = out[:half]
                corner_give[...] = out[half:]
            else:
                keep_ref[g + 2 * side] = out[:half]
                give_ref[g + 2 * side] = out[half:]


def run_experts(places, weights, groups, block, room, first):
    experts, model, hidden = weights[0].shape
    width = model // 2
    rows = 2 * sum(piece.shape[0] for piece in groups[0][0])
    table = groups[0][0][0].shape[1] - width
    where = pltpu.HBM if first else pltpu.VMEM
    operands = [pltpu.with_memory_space_constraint(w, where) for w in weights]
    operands += [near(piece) for pair in groups for half in pair for piece in half]
    outs = [jax.ShapeDtypeStruct((rows // 4, width), BF16)] * 2
    outs += [jax.ShapeDtypeStruct((3, rows // 4, width), BF16)] * 2
    extra = []
    if first:
        outs += [jax.ShapeDtypeStruct(w.shape, BF16) for w in weights]
        extra = [pltpu.SemaphoreType.DMA((3 * experts,))]
    slots = rows // 2 // block * room
    counts = tuple(tuple(len(half) for half in pair) for pair in groups)
    return pl.pallas_call(
        functools.partial(experts_kernel, first, counts, block, room),
        in_specs=[pl.BlockSpec(memory_space=pltpu.SMEM)]
        + [pl.BlockSpec(memory_space=pl.ANY if first else pltpu.VMEM)] * 3
        + [VMEM_SPEC] * (len(operands) - 3),
        out_specs=[VMEM_SPEC] * len(outs),
        scratch_shapes=[
            pltpu.VMEM((rows, model), BF16),
            pltpu.VMEM((rows, table), F32),
            pltpu.VMEM((2, rows // 2, experts * slots), BF16),
            pltpu.VMEM((experts, 2 * slots, model), BF16),
            pltpu.VMEM((2, experts * slots, model), BF16),
            pltpu.VMEM((experts, 2 * slots, hidden), BF16),
        ]
        + extra,
        out_shape=outs,
        compiler_params=pltpu.CompilerParams(vmem_limit_bytes=20 * MIB),
        cost_estimate=pl.CostEstimate(flops=rows, bytes_accessed=rows, transcendentals=0),
    )(places, *operands)


def cut_kernel(by_x, by_y, *refs):
    out_x, out_y = refs[-2:]
    half = out_x.shape[0]
    out_x[...] = by_x[:half, : out_x.shape[1]]
    out_y[...] = by_y[half:]


def cut(by_x, by_y, behind):
    half = jax.ShapeDtypeStruct((by_y.shape[0] // 2, by_y.shape[1]), BF16)
    return pl.pallas_call(
        cut_kernel,
        in_specs=[VMEM_SPEC] * 2 + [pl.BlockSpec(memory_space=pl.ANY)] * len(behind),
        out_specs=[VMEM_SPEC] * 2,
        out_shape=[half, half],
        compiler_params=pltpu.CompilerParams(vmem_limit_bytes=2 * MIB),
        cost_estimate=pl.CostEstimate(flops=1, bytes_accessed=1, transcendentals=0),
    )(near(by_x), near(by_y), *behind)


def add(*terms):
    return functools.reduce(lambda a, b: a + b, [t.astype(F32) for t in terms]).astype(BF16)


def after(arrays, others):
    return lax.optimization_barrier((arrays, others))[0]


def planned(peers, tokens, expert_ids, route_weights, w_gate, w_up, w_down):
    line = peers // 4

    def send(array, steps=0, x=0, core=0, y=0):
        pairs = []
        for side in range(2):
            for e in range(peers):
                to = ((e // 4) ^ steps) * 4 + ((e // 2 % 2) ^ x) * 2 + ((e % 2) ^ core)
                pairs.append((side * peers + e, (side ^ y) * peers + to))
        return lax.ppermute(array, PAIR, pairs)

    expert_count = peers * w_gate.shape[0]
    columns = -(-expert_count // LANES) * LANES
    places = jnp.stack([lax.axis_index("dp"), lax.axis_index("expert")]).astype(jnp.int32)
    rows = pack(tokens, expert_ids, route_weights, columns)

    def join(pieces):
        return jnp.concatenate(pieces, 0)

    def cores(pieces):
        return [send(piece, core=1) for piece in pieces]

    def gather(own, direct):
        features = own[:, : tokens.shape[1]]
        by_x, by_y = send(own, x=1), send(features, y=1)
        if direct:
            corner = [send(features, x=1, y=1)]
        else:
            half_x, half_y = cut(by_x, by_y, [])
            corner = [send(half_x, y=1), send(half_y, x=1)]
        return [[own] + cores([own]), [by_y] + cores([by_y])], [[by_x] + cores([by_x]), corner + cores(corner)]

    def total(keep, give):
        return add(keep, send(give, core=1))

    def turn(corner, rest):
        for_x, for_y = rest[1], rest[2]
        half = for_x.shape[0] // 2
        got_a, got_b = send(corner[:half], x=1), send(corner[half:], y=1)
        for_x = join([for_x[:half], add(for_x[half:], got_b)])
        for_y = join([add(for_y[:half], got_a), for_y[half:]])
        return for_x, for_y

    weights = (w_gate, w_up, w_down.reshape(-1, w_down.shape[2]))
    block = tokens.shape[0]
    room = block * expert_ids.shape[1] * 3 // (2 * expert_count)
    blocks = [rows] + [send(rows, steps=k) for k in range(1, line)]
    parts, first, sums = 2, True, []
    count = line // parts
    for i in range(parts):
        groups = gather(join(blocks[i * count : (i + 1) * count]), GATHER[i])
        corner, corner_give, keep, give, *rest = run_experts(places, weights, groups, block, room, first)
        if first:
            weights, first = rest, False
        rest = total(keep, give)
        corner = total(corner, corner_give)
        if SCATTER[i]:
            sums.append((rest[0], rest[1], rest[2], [send(corner, x=1, y=1)]))
        else:
            sums.append((rest[0], *turn(corner, rest), []))
    back, arrived = [], ()
    for i in reversed(range(parts)):
        own, for_x, for_y, direct = sums[i]
        for_x, for_y = after((for_x, for_y), arrived)
        arrived = send(for_x, x=1), send(for_y, y=1)
        mine = add(own, *arrived, *direct)
        for k in reversed(range(count)):
            piece = mine[k * block : (k + 1) * block]
            back.append(send(piece, steps=i * count + k) if i or k else piece)
    return add(*back)


def general(tokens, expert_ids, route_weights, w_gate, w_up, w_down):
    peers, local = lax.axis_size("expert"), w_gate.shape[0]
    table = route_table(expert_ids, route_weights, peers * local).astype(BF16)
    rows = lax.all_gather(tokens, "expert", axis=0, tiled=True)
    rows = lax.all_gather(rows, "dp", axis=1, tiled=True)
    table = lax.all_gather(table, "expert", axis=0, tiled=True).astype(F32)
    weight = lax.dynamic_slice_in_dim(table, lax.axis_index("expert") * local, local, 1)
    gate = jnp.einsum("td,rdf->trf", rows, w_gate, preferred_element_type=F32)
    up = jnp.einsum("td,rdf->trf", rows, w_up, preferred_element_type=F32)
    hidden = (jax.nn.silu(gate) * up * weight[:, :, None]).astype(BF16)
    out = jnp.einsum("trf,rfd->td", hidden, w_down, preferred_element_type=F32).astype(BF16)
    out = lax.psum_scatter(out, "dp", scatter_dimension=1, tiled=True)
    return lax.psum_scatter(out, "expert", scatter_dimension=0, tiled=True)


def solution(mesh):
    peers = mesh.shape["expert"]
    body = general
    if mesh.shape["dp"] == 2 and peers % 8 == 0 and peers & (peers - 1) == 0:
        body = functools.partial(planned, peers)
    return jax.shard_map(
        body,
        mesh=mesh,
        in_specs=(
            P("expert", "dp"),
            P("expert", None),
            P("expert", None),
            P("expert", None, "dp"),
            P("expert", None, "dp"),
            P("expert", "dp", None),
        ),
        out_specs=P("expert", "dp"),
        check_vma=False,
    )
```

```python
import functools

import jax
import jax.numpy as jnp
from jax import lax
from jax.experimental import pallas as pl
from jax.experimental.pallas import tpu as pltpu
from jax.sharding import PartitionSpec as P

BF16, F32 = jnp.bfloat16, jnp.float32
PAIR = ("dp", "expert")
LANES = 128
GATHER = (True, False)
SCATTER = (False, False)
MIB = 1024 * 1024
VMEM_SPEC = pl.BlockSpec(memory_space=pltpu.VMEM)


def near(array):
    return pltpu.with_memory_space_constraint(array, pltpu.VMEM)


def route_table(ids, weights, experts):
    lane = lax.broadcasted_iota(jnp.int32, (ids.shape[0], experts), 1)
    table = jnp.zeros((ids.shape[0], experts), F32)
    for k in range(ids.shape[1]):
        table = table + jnp.where(ids[:, k : k + 1] == lane, weights[:, k : k + 1].astype(F32), 0.0)
    return table


def pack_kernel(tok_hbm, ids_hbm, rw_hbm, out_ref, ids_ref, rw_ref, sem):
    rows, width = tok_hbm.shape
    columns = out_ref.shape[1] - width
    ends = (ids_hbm, ids_ref), (rw_hbm, rw_ref), (tok_hbm, out_ref.at[:, pl.ds(0, width)])
    copies = [pltpu.make_async_copy(*pair, sem.at[i]) for i, pair in enumerate(ends)]
    for copy in copies:
        copy.start()
    for copy in copies[:2]:
        copy.wait()
    line = lax.broadcasted_iota(jnp.int32, (columns, rows), 0)
    table = jnp.zeros((columns, rows), F32)
    for k in range(ids_ref.shape[0]):
        table = table + jnp.where(ids_ref[k : k + 1, :] == line, rw_ref[k : k + 1, :].astype(F32), 0.0)
    out_ref[:, width:] = table.T.astype(BF16)
    copies[2].wait()


def pack(tokens, ids, route_weights, columns):
    rows, width = tokens.shape
    operands = [pltpu.with_memory_space_constraint(x, pltpu.HBM) for x in (tokens, ids.T, route_weights.T)]
    return pl.pallas_call(
        pack_kernel,
        in_specs=[pl.BlockSpec(memory_space=pl.ANY)] * 3,
        out_specs=VMEM_SPEC,
        out_shape=jax.ShapeDtypeStruct((rows, width + columns), BF16),
        scratch_shapes=[
            pltpu.VMEM(operands[1].shape, jnp.int32),
            pltpu.VMEM(operands[2].shape, BF16),
            pltpu.SemaphoreType.DMA((3,)),
        ],
        compiler_params=pltpu.CompilerParams(vmem_limit_bytes=2 * MIB),
    )(*operands)


def earlier(rows, block):
    this = lax.broadcasted_iota(jnp.int32, (rows, rows), 0)
    other = lax.broadcasted_iota(jnp.int32, (rows, rows), 1)
    start = jnp.zeros((rows, 1), jnp.int32)
    place = lax.broadcasted_iota(jnp.int32, (rows, 1), 0)
    for i in range(1, rows // block):
        start = jnp.where(place >= i * block, i * block, start)
    return ((other < this) & (other >= start)).astype(BF16)


def dispatch(table, before, expert_place, experts, block, room):
    rows = table.shape[0]
    ranks = jnp.dot(before, (table > 0.0).astype(BF16), preferred_element_type=F32)
    lane = lax.broadcasted_iota(jnp.int32, table.shape, 1)
    slots = experts * rows // block * room
    slot = lax.broadcasted_iota(jnp.int32, (rows, slots), 1)
    place = lax.broadcasted_iota(jnp.int32, (rows, 1), 0)
    first = jnp.zeros((rows, 1), jnp.int32)
    for i in range(1, rows // block):
        first = jnp.where(place >= i * block, i * room, first)
    taken = jnp.zeros((rows, slots), F32)
    for e in range(experts):
        here = lane == expert_place * experts + e
        weight = jnp.sum(jnp.where(here, table, 0.0), axis=1, keepdims=True)
        rank = jnp.sum(jnp.where(here, ranks, 0.0), axis=1, keepdims=True).astype(jnp.int32)
        taken = taken + jnp.where(slot == first + rank + e * (slots // experts), weight, 0.0)
    return taken


def experts_kernel(first, counts, block, room, places, gate_in, up_in, down_in, *refs):
    if first:
        pieces, refs = refs[:-14], refs[-14:]
        corner_keep, corner_give, keep_ref, give_ref, gate_ref, up_ref, down_ref, *refs, sem = refs
    else:
        pieces, refs = refs[:-10], refs[-10:]
        corner_keep, corner_give, keep_ref, give_ref, *refs = refs
        gate_ref, up_ref, down_ref = gate_in, up_in, down_in
    rows_buf, table_buf, taken_buf, packed_buf, out_buf, hidden_buf = refs
    experts, model, hidden = gate_ref.shape
    width = model // 2
    fetches = []
    if first:
        ends = []
        for e in range(experts):
            ends += [(gate_in.at[e], gate_ref.at[e]), (up_in.at[e], up_ref.at[e])]
        for e in range(experts):
            span = pl.ds(e * hidden, hidden)
            ends += [(down_in.at[span], down_ref.at[span])]
        fetches = [pltpu.make_async_copy(*pair, sem.at[i]) for i, pair in enumerate(ends)]
        for copy in fetches:
            copy.start()

    mine = pl.ds(pl.multiple_of(places[0] * width, width), width)
    others = pl.ds(pl.multiple_of((1 - places[0]) * width, width), width)
    group = rows_buf.shape[0] // 2
    slots = taken_buf.shape[2] // experts
    before = earlier(group, block)
    taken = 0
    for g in range(2):
        for count, columns in zip(counts[g], (mine, others)):
            row = g * group
            for piece in pieces[taken : taken + count]:
                span = pl.ds(row, piece.shape[0])
                rows_buf[span, columns] = piece[:, :width]
                if columns is mine:
                    table_buf[span, :] = piece[:, width:].astype(F32)
                row += piece.shape[0]
            taken += count
        table = dispatch(table_buf[pl.ds(g * group, group), :], before, places[1], experts, block, room)
        taken_buf[g] = table.astype(BF16)
        picked = jnp.where(table > 0.0, 1.0, 0.0).T.astype(BF16)
        packed = jnp.dot(picked, rows_buf[pl.ds(g * group, group), :], preferred_element_type=F32).astype(BF16)
        for e in range(experts):
            packed_buf[e, pl.ds(g * slots, slots), :] = packed[e * slots : (e + 1) * slots]

    for e in range(experts):
        for copy in fetches[2 * e : 2 * e + 2]:
            copy.wait()
        rows = packed_buf[e]
        gate = jnp.dot(rows, gate_ref[e], preferred_element_type=F32)
        up = jnp.dot(rows, up_ref[e], preferred_element_type=F32)
        hidden_buf[e] = (gate / (1.0 + jnp.exp(-gate)) * up).astype(BF16)
    for e in range(experts):
        for copy in fetches[2 * experts + e : 2 * experts + e + 1]:
            copy.wait()
        down = down_ref[pl.ds(e * hidden, hidden), :]
        out = jnp.dot(hidden_buf[e], down, preferred_element_type=F32).astype(BF16)
        for g in range(2):
            out_buf[g, pl.ds(e * slots, slots), :] = out[g * slots : (g + 1) * slots]
    half = group // 2
    for g in (1, 0):
        for side, columns in enumerate((mine, others)):
            out = jnp.dot(taken_buf[g], out_buf[g, :, columns], preferred_element_type=F32).astype(BF16)
            if g and side:
                corner_keep[...] = out[:half]
                corner_give[...] = out[half:]
            else:
                keep_ref[g + 2 * side] = out[:half]
                give_ref[g + 2 * side] = out[half:]


def run_experts(places, weights, groups, block, room, first):
    experts, model, hidden = weights[0].shape
    width = model // 2
    rows = 2 * sum(piece.shape[0] for piece in groups[0][0])
    table = groups[0][0][0].shape[1] - width
    where = pltpu.HBM if first else pltpu.VMEM
    operands = [pltpu.with_memory_space_constraint(w, where) for w in weights]
    operands += [near(piece) for pair in groups for half in pair for piece in half]
    outs = [jax.ShapeDtypeStruct((rows // 4, width), BF16)] * 2
    outs += [jax.ShapeDtypeStruct((3, rows // 4, width), BF16)] * 2
    extra = []
    if first:
        outs += [jax.ShapeDtypeStruct(w.shape, BF16) for w in weights]
        extra = [pltpu.SemaphoreType.DMA((3 * experts,))]
    slots = rows // 2 // block * room
    counts = tuple(tuple(len(half) for half in pair) for pair in groups)
    return pl.pallas_call(
        functools.partial(experts_kernel, first, counts, block, room),
        in_specs=[pl.BlockSpec(memory_space=pltpu.SMEM)]
        + [pl.BlockSpec(memory_space=pl.ANY if first else pltpu.VMEM)] * 3
        + [VMEM_SPEC] * (len(operands) - 3),
        out_specs=[VMEM_SPEC] * len(outs),
        scratch_shapes=[
            pltpu.VMEM((rows, model), BF16),
            pltpu.VMEM((rows, table), F32),
            pltpu.VMEM((2, rows // 2, experts * slots), BF16),
            pltpu.VMEM((experts, 2 * slots, model), BF16),
            pltpu.VMEM((2, experts * slots, model), BF16),
            pltpu.VMEM((experts, 2 * slots, hidden), BF16),
        ]
        + extra,
        out_shape=outs,
        compiler_params=pltpu.CompilerParams(vmem_limit_bytes=20 * MIB),
        cost_estimate=pl.CostEstimate(flops=rows, bytes_accessed=rows, transcendentals=0),
    )(places, *operands)


def add(*terms):
    return functools.reduce(lambda a, b: a + b, [t.astype(F32) for t in terms]).astype(BF16)


def after(arrays, others):
    return lax.optimization_barrier((arrays, others))[0]


def planned(peers, tokens, expert_ids, route_weights, w_gate, w_up, w_down):
    line = peers // 4

    def send(array, steps=0, x=0, core=0, y=0):
        pairs = []
        for side in range(2):
            for e in range(peers):
                to = ((e // 4) ^ steps) * 4 + ((e // 2 % 2) ^ x) * 2 + ((e % 2) ^ core)
                pairs.append((side * peers + e, (side ^ y) * peers + to))
        return lax.ppermute(array, PAIR, pairs)

    expert_count = peers * w_gate.shape[0]
    columns = -(-expert_count // LANES) * LANES
    places = jnp.stack([lax.axis_index("dp"), lax.axis_index("expert")]).astype(jnp.int32)
    rows = pack(tokens, expert_ids, route_weights, columns)

    def join(pieces):
        return jnp.concatenate(pieces, 0)

    def cores(pieces):
        return [send(piece, core=1) for piece in pieces]

    def gather(own, direct):
        features = own[:, : tokens.shape[1]]
        by_x, by_y = send(own, x=1), send(features, y=1)
        if direct:
            corner = [send(features, x=1, y=1)]
        else:
            half = by_y.shape[0] // 2
            half_x, half_y = by_x[:half, : tokens.shape[1]], by_y[half:]
            corner = [send(half_x, y=1), send(half_y, x=1)]
        return [[own] + cores([own]), [by_y] + cores([by_y])], [[by_x] + cores([by_x]), corner + cores(corner)]

    def total(keep, give):
        return add(keep, send(give, core=1))

    def turn(corner, rest):
        for_x, for_y = rest[1], rest[2]
        half = for_x.shape[0] // 2
        got_a, got_b = send(corner[:half], x=1), send(corner[half:], y=1)
        for_x = join([for_x[:half], add(for_x[half:], got_b)])
        for_y = join([add(for_y[:half], got_a), for_y[half:]])
        return for_x, for_y

    weights = (w_gate, w_up, w_down.reshape(-1, w_down.shape[2]))
    block = tokens.shape[0]
    room = block * expert_ids.shape[1] * 3 // (2 * expert_count)
    blocks = [rows] + [send(rows, steps=k) for k in range(1, line)]
    parts, first, sums = 2, True, []
    count = line // parts
    for i in range(parts):
        groups = gather(join(blocks[i * count : (i + 1) * count]), GATHER[i])
        corner, corner_give, keep, give, *rest = run_experts(places, weights, groups, block, room, first)
        if first:
            weights, first = rest, False
        rest = total(keep, give)
        corner = total(corner, corner_give)
        if SCATTER[i]:
            sums.append((rest[0], rest[1], rest[2], [send(corner, x=1, y=1)]))
        else:
            sums.append((rest[0], *turn(corner, rest), []))
    back, arrived = [], ()
    for i in reversed(range(parts)):
        own, for_x, for_y, direct = sums[i]
        if arrived:
            for_y = after(for_y, arrived[0])
            for_x = after(for_x, arrived[1])
        arrived = send(for_x, x=1), send(for_y, y=1)
        mine = add(own, *arrived, *direct)
        for k in reversed(range(count)):
            piece = mine[k * block : (k + 1) * block]
            back.append(send(piece, steps=i * count + k) if i or k else piece)
    return add(*back)


def general(tokens, expert_ids, route_weights, w_gate, w_up, w_down):
    peers, local = lax.axis_size("expert"), w_gate.shape[0]
    table = route_table(expert_ids, route_weights, peers * local).astype(BF16)
    rows = lax.all_gather(tokens, "expert", axis=0, tiled=True)
    rows = lax.all_gather(rows, "dp", axis=1, tiled=True)
    table = lax.all_gather(table, "expert", axis=0, tiled=True).astype(F32)
    weight = lax.dynamic_slice_in_dim(table, lax.axis_index("expert") * local, local, 1)
    gate = jnp.einsum("td,rdf->trf", rows, w_gate, preferred_element_type=F32)
    up = jnp.einsum("td,rdf->trf", rows, w_up, preferred_element_type=F32)
    hidden = (jax.nn.silu(gate) * up * weight[:, :, None]).astype(BF16)
    out = jnp.einsum("trf,rfd->td", hidden, w_down, preferred_element_type=F32).astype(BF16)
    out = lax.psum_scatter(out, "dp", scatter_dimension=1, tiled=True)
    return lax.psum_scatter(out, "expert", scatter_dimension=0, tiled=True)


def solution(mesh):
    peers = mesh.shape["expert"]
    body = general
    if mesh.shape["dp"] == 2 and peers % 8 == 0 and peers & (peers - 1) == 0:
        body = functools.partial(planned, peers)
    return jax.shard_map(
        body,
        mesh=mesh,
        in_specs=(
            P("expert", "dp"),
            P("expert", None),
            P("expert", None),
            P("expert", None, "dp"),
            P("expert", None, "dp"),
            P("expert", "dp", None),
        ),
        out_specs=P("expert", "dp"),
        check_vma=False,
    )
```

```python
import functools

import jax
import jax.numpy as jnp
from jax import lax
from jax.experimental import pallas as pl
from jax.experimental.pallas import tpu as pltpu
from jax.sharding import PartitionSpec as P

BF16, F32 = jnp.bfloat16, jnp.float32
PAIR = ("dp", "expert")
LANES = 128
GATHER = (True, False)
SCATTER = (False, False)
MIB = 1024 * 1024
VMEM_SPEC = pl.BlockSpec(memory_space=pltpu.VMEM)


def near(array):
    return pltpu.with_memory_space_constraint(array, pltpu.VMEM)


def route_table(ids, weights, experts):
    lane = lax.broadcasted_iota(jnp.int32, (ids.shape[0], experts), 1)
    table = jnp.zeros((ids.shape[0], experts), F32)
    for k in range(ids.shape[1]):
        table = table + jnp.where(ids[:, k : k + 1] == lane, weights[:, k : k + 1].astype(F32), 0.0)
    return table


def pack_kernel(tok_hbm, ids_hbm, rw_hbm, out_ref, ids_ref, rw_ref, sem):
    rows, width = tok_hbm.shape
    columns = out_ref.shape[1] - width
    ends = (ids_hbm, ids_ref), (rw_hbm, rw_ref), (tok_hbm, out_ref.at[:, pl.ds(0, width)])
    copies = [pltpu.make_async_copy(*pair, sem.at[i]) for i, pair in enumerate(ends)]
    for copy in copies:
        copy.start()
    for copy in copies[:2]:
        copy.wait()
    line = lax.broadcasted_iota(jnp.int32, (columns, rows), 0)
    table = jnp.zeros((columns, rows), F32)
    for k in range(ids_ref.shape[0]):
        table = table + jnp.where(ids_ref[k : k + 1, :] == line, rw_ref[k : k + 1, :].astype(F32), 0.0)
    out_ref[:, width:] = table.T.astype(BF16)
    copies[2].wait()


def pack(tokens, ids, route_weights, columns):
    rows, width = tokens.shape
    operands = [pltpu.with_memory_space_constraint(x, pltpu.HBM) for x in (tokens, ids.T, route_weights.T)]
    return pl.pallas_call(
        pack_kernel,
        in_specs=[pl.BlockSpec(memory_space=pl.ANY)] * 3,
        out_specs=VMEM_SPEC,
        out_shape=jax.ShapeDtypeStruct((rows, width + columns), BF16),
        scratch_shapes=[
            pltpu.VMEM(operands[1].shape, jnp.int32),
            pltpu.VMEM(operands[2].shape, BF16),
            pltpu.SemaphoreType.DMA((3,)),
        ],
        compiler_params=pltpu.CompilerParams(vmem_limit_bytes=2 * MIB),
    )(*operands)


def earlier(rows, block):
    this = lax.broadcasted_iota(jnp.int32, (rows, rows), 0)
    other = lax.broadcasted_iota(jnp.int32, (rows, rows), 1)
    start = jnp.zeros((rows, 1), jnp.int32)
    place = lax.broadcasted_iota(jnp.int32, (rows, 1), 0)
    for i in range(1, rows // block):
        start = jnp.where(place >= i * block, i * block, start)
    return ((other < this) & (other >= start)).astype(BF16)


def dispatch(table, before, expert_place, experts, block, room):
    rows = table.shape[0]
    ranks = jnp.dot(before, (table > 0.0).astype(BF16), preferred_element_type=F32)
    lane = lax.broadcasted_iota(jnp.int32, table.shape, 1)
    slots = experts * rows // block * room
    slot = lax.broadcasted_iota(jnp.int32, (rows, slots), 1)
    place = lax.broadcasted_iota(jnp.int32, (rows, 1), 0)
    first = jnp.zeros((rows, 1), jnp.int32)
    for i in range(1, rows // block):
        first = jnp.where(place >= i * block, i * room, first)
    taken = jnp.zeros((rows, slots), F32)
    for e in range(experts):
        here = lane == expert_place * experts + e
        weight = jnp.sum(jnp.where(here, table, 0.0), axis=1, keepdims=True)
        rank = jnp.sum(jnp.where(here, ranks, 0.0), axis=1, keepdims=True).astype(jnp.int32)
        taken = taken + jnp.where(slot == first + rank + e * (slots // experts), weight, 0.0)
    return taken


def experts_kernel(first, counts, block, room, places, gate_in, up_in, down_in, *refs):
    if first:
        pieces, refs = refs[:-14], refs[-14:]
        corner_keep, corner_give, keep_ref, give_ref, gate_ref, up_ref, down_ref, *refs, sem = refs
    else:
        pieces, refs = refs[:-10], refs[-10:]
        corner_keep, corner_give, keep_ref, give_ref, *refs = refs
        gate_ref, up_ref, down_ref = gate_in, up_in, down_in
    rows_buf, table_buf, taken_buf, packed_buf, out_buf, hidden_buf = refs
    experts, model, hidden = gate_ref.shape
    width = model // 2
    fetches = []
    if first:
        ends = []
        for e in range(experts):
            ends += [(gate_in.at[e], gate_ref.at[e]), (up_in.at[e], up_ref.at[e])]
        for e in range(experts):
            span = pl.ds(e * hidden, hidden)
            ends += [(down_in.at[span], down_ref.at[span])]
        fetches = [pltpu.make_async_copy(*pair, sem.at[i]) for i, pair in enumerate(ends)]
        for copy in fetches:
            copy.start()

    mine = pl.ds(pl.multiple_of(places[0] * width, width), width)
    others = pl.ds(pl.multiple_of((1 - places[0]) * width, width), width)
    group = rows_buf.shape[0] // 2
    slots = taken_buf.shape[2] // experts
    before = earlier(group, block)
    taken = 0
    for g in range(2):
        for count, columns in zip(counts[g], (mine, others)):
            row = g * group
            for piece in pieces[taken : taken + count]:
                span = pl.ds(row, piece.shape[0])
                rows_buf[span, columns] = piece[:, :width]
                if columns is mine:
                    table_buf[span, :] = piece[:, width:].astype(F32)
                row += piece.shape[0]
            taken += count
        table = dispatch(table_buf[pl.ds(g * group, group), :], before, places[1], experts, block, room)
        taken_buf[g] = table.astype(BF16)
        picked = jnp.where(table > 0.0, 1.0, 0.0).T.astype(BF16)
        packed = jnp.dot(picked, rows_buf[pl.ds(g * group, group), :], preferred_element_type=F32).astype(BF16)
        for e in range(experts):
            packed_buf[e, pl.ds(g * slots, slots), :] = packed[e * slots : (e + 1) * slots]

    for e in range(experts):
        for copy in fetches[2 * e : 2 * e + 2]:
            copy.wait()
        rows = packed_buf[e]
        gate = jnp.dot(rows, gate_ref[e], preferred_element_type=F32)
        up = jnp.dot(rows, up_ref[e], preferred_element_type=F32)
        hidden_buf[e] = (gate / (1.0 + jnp.exp(-gate)) * up).astype(BF16)
    for e in range(experts):
        for copy in fetches[2 * experts + e : 2 * experts + e + 1]:
            copy.wait()
        down = down_ref[pl.ds(e * hidden, hidden), :]
        out = jnp.dot(hidden_buf[e], down, preferred_element_type=F32).astype(BF16)
        for g in range(2):
            out_buf[g, pl.ds(e * slots, slots), :] = out[g * slots : (g + 1) * slots]
    half = group // 2
    for g in (1, 0):
        for side, columns in enumerate((mine, others)):
            out = jnp.dot(taken_buf[g], out_buf[g, :, columns], preferred_element_type=F32).astype(BF16)
            if g and side:
                corner_keep[...] = out[:half]
                corner_give[...] = out[half:]
            else:
                keep_ref[g + 2 * side] = out[:half]
                give_ref[g + 2 * side] = out[half:]


def run_experts(places, weights, groups, block, room, first):
    experts, model, hidden = weights[0].shape
    width = model // 2
    rows = 2 * sum(piece.shape[0] for piece in groups[0][0])
    table = groups[0][0][0].shape[1] - width
    where = pltpu.HBM if first else pltpu.VMEM
    operands = [pltpu.with_memory_space_constraint(w, where) for w in weights]
    operands += [near(piece) for pair in groups for half in pair for piece in half]
    outs = [jax.ShapeDtypeStruct((rows // 4, width), BF16)] * 2
    outs += [jax.ShapeDtypeStruct((3, rows // 4, width), BF16)] * 2
    extra = []
    if first:
        outs += [jax.ShapeDtypeStruct(w.shape, BF16) for w in weights]
        extra = [pltpu.SemaphoreType.DMA((3 * experts,))]
    slots = rows // 2 // block * room
    counts = tuple(tuple(len(half) for half in pair) for pair in groups)
    return pl.pallas_call(
        functools.partial(experts_kernel, first, counts, block, room),
        in_specs=[pl.BlockSpec(memory_space=pltpu.SMEM)]
        + [pl.BlockSpec(memory_space=pl.ANY if first else pltpu.VMEM)] * 3
        + [VMEM_SPEC] * (len(operands) - 3),
        out_specs=[VMEM_SPEC] * len(outs),
        scratch_shapes=[
            pltpu.VMEM((rows, model), BF16),
            pltpu.VMEM((rows, table), F32),
            pltpu.VMEM((2, rows // 2, experts * slots), BF16),
            pltpu.VMEM((experts, 2 * slots, model), BF16),
            pltpu.VMEM((2, experts * slots, model), BF16),
            pltpu.VMEM((experts, 2 * slots, hidden), BF16),
        ]
        + extra,
        out_shape=outs,
        compiler_params=pltpu.CompilerParams(vmem_limit_bytes=20 * MIB),
        cost_estimate=pl.CostEstimate(flops=rows, bytes_accessed=rows, transcendentals=0),
    )(places, *operands)


def add(*terms):
    return functools.reduce(lambda a, b: a + b, [t.astype(F32) for t in terms]).astype(BF16)


def after(arrays, others):
    return lax.optimization_barrier((arrays, others))[0]


def planned(peers, tokens, expert_ids, route_weights, w_gate, w_up, w_down):
    line = peers // 4

    def send(array, steps=0, x=0, core=0, y=0):
        pairs = []
        for side in range(2):
            for e in range(peers):
                to = ((e // 4) ^ steps) * 4 + ((e // 2 % 2) ^ x) * 2 + ((e % 2) ^ core)
                pairs.append((side * peers + e, (side ^ y) * peers + to))
        return lax.ppermute(array, PAIR, pairs)

    expert_count = peers * w_gate.shape[0]
    columns = -(-expert_count // LANES) * LANES
    places = jnp.stack([lax.axis_index("dp"), lax.axis_index("expert")]).astype(jnp.int32)
    rows = pack(tokens, expert_ids, route_weights, columns)

    def join(pieces):
        return jnp.concatenate(pieces, 0)

    def cores(pieces):
        return [send(piece, core=1) for piece in pieces]

    def gather(own, direct):
        features = own[:, : tokens.shape[1]]
        by_x, by_y = send(own, x=1), send(features, y=1)
        if direct:
            corner = [send(features, x=1, y=1)]
        else:
            half = by_y.shape[0] // 2
            half_x, half_y = by_x[:half, : tokens.shape[1]], by_y[half:]
            corner = [send(half_x, y=1), send(half_y, x=1)]
        return [[own] + cores([own]), [by_y] + cores([by_y])], [[by_x] + cores([by_x]), corner + cores(corner)]

    def total(keep, give):
        return add(keep, send(give, core=1))

    def turn(corner, rest):
        for_x, for_y = rest[1], rest[2]
        half = for_x.shape[0] // 2
        got_b, got_a = send(corner[half:], y=1), send(corner[:half], x=1)
        for_x = join([for_x[:half], add(for_x[half:], got_b)])
        for_y = join([add(for_y[:half], got_a), for_y[half:]])
        return for_x, for_y

    weights = (w_gate, w_up, w_down.reshape(-1, w_down.shape[2]))
    block = tokens.shape[0]
    room = block * expert_ids.shape[1] * 3 // (2 * expert_count)
    blocks = [rows] + [send(rows, steps=k) for k in range(1, line)]
    parts, first, sums = 2, True, []
    count = line // parts
    for i in range(parts):
        groups = gather(join(blocks[i * count : (i + 1) * count]), GATHER[i])
        corner, corner_give, keep, give, *rest = run_experts(places, weights, groups, block, room, first)
        if first:
            weights, first = rest, False
        rest = total(keep, give)
        corner = total(corner, corner_give)
        if SCATTER[i]:
            sums.append((rest[0], rest[1], rest[2], [send(corner, x=1, y=1)]))
        else:
            sums.append((rest[0], *turn(corner, rest), []))
    back, arrived = [], ()
    for i in reversed(range(parts)):
        own, for_x, for_y, direct = sums[i]
        if arrived:
            for_y = after(for_y, arrived[0])
            for_x = after(for_x, arrived[1])
        arrived = send(for_x, x=1), send(for_y, y=1)
        mine = add(own, *arrived, *direct)
        for k in reversed(range(count)):
            piece = mine[k * block : (k + 1) * block]
            back.append(send(piece, steps=i * count + k) if i or k else piece)
    return add(*back)


def general(tokens, expert_ids, route_weights, w_gate, w_up, w_down):
    peers, local = lax.axis_size("expert"), w_gate.shape[0]
    table = route_table(expert_ids, route_weights, peers * local).astype(BF16)
    rows = lax.all_gather(tokens, "expert", axis=0, tiled=True)
    rows = lax.all_gather(rows, "dp", axis=1, tiled=True)
    table = lax.all_gather(table, "expert", axis=0, tiled=True).astype(F32)
    weight = lax.dynamic_slice_in_dim(table, lax.axis_index("expert") * local, local, 1)
    gate = jnp.einsum("td,rdf->trf", rows, w_gate, preferred_element_type=F32)
    up = jnp.einsum("td,rdf->trf", rows, w_up, preferred_element_type=F32)
    hidden = (jax.nn.silu(gate) * up * weight[:, :, None]).astype(BF16)
    out = jnp.einsum("trf,rfd->td", hidden, w_down, preferred_element_type=F32).astype(BF16)
    out = lax.psum_scatter(out, "dp", scatter_dimension=1, tiled=True)
    return lax.psum_scatter(out, "expert", scatter_dimension=0, tiled=True)


def solution(mesh):
    peers = mesh.shape["expert"]
    body = general
    if mesh.shape["dp"] == 2 and peers % 8 == 0 and peers & (peers - 1) == 0:
        body = functools.partial(planned, peers)
    return jax.shard_map(
        body,
        mesh=mesh,
        in_specs=(
            P("expert", "dp"),
            P("expert", None),
            P("expert", None),
            P("expert", None, "dp"),
            P("expert", None, "dp"),
            P("expert", "dp", None),
        ),
        out_specs=P("expert", "dp"),
        check_vma=False,
    )
```
